32 devices in a mesh: grp: 2 (over x), layer: 16 (over z, y, core).
Axes of the slice: x: 2, y: 2, z: 4, core: 2. Of those that a mesh axis runs over, the one named last changes fastest.
Arguments:
- query_pool: bfloat16 [1024, 16, 4096], P('grp', 'layer'), parts along dimension 0, may hold values from -6 to 6
- train_store: bfloat16 [2048, 16, 4096], P('grp', 'layer'), parts along dimension 0, may hold values from -6 to 6
- query_ids: int32 [1024], P('grp'), parts along dimension 0, may hold values from 0 to 511
- train_ids: int32 [2048], P('grp'), parts along dimension 0, may hold values from 0 to 1023
- out_basis: bfloat16 [16, 64, 64], P('layer'), may hold values from -0.75 to 0.75
- in_basis: bfloat16 [16, 64, 64], P('layer'), may hold values from -0.75 to 0.75
- eigenvalues: float32 [16, 4096], P('layer'), may hold values from 0.05 to 100
Outputs:
- scores: float32 [1024, 1024], P('grp', 'layer'), parts along dimension 0
The draws below stay inside these ranges and needn't reach their ends.
There are 2 independent parts, one for each index of `grp`. The reference program is written for one: setup_inputs(seed, part) draws one part's arguments, and reference() takes and returns one part's arrays. A program takes and returns all parts, laid end to end along the dimension named above; an argument that names none is the same for every part. Nothing has to cross between parts.
All inputs are finite; a program needn't handle non-finite values.
Results may differ from the reference program's by a relative error of at most 0.0042.
Values sent between devices are 32-bit elements; how exact they have to be, the bound alone decides.
No kernel may reach another device: no remote copies, remote signals or barrier semaphores. Data moves between devices by JAX's collectives and lax.ppermute only.
A program may use at most 128 MiB of HBM per device.

```python
import jax
import jax.numpy as jnp
from jax import lax

OUT = 64
IN = 64
FEAT = 4096
MODULES = 16
QUERIES = 512
TRAIN = 1024


def draw_eigenvalues(key, part):
    key = jax.random.fold_in(key, 7)
    ramp = jnp.arange(MODULES, dtype=jnp.float32)[:, None] / max(MODULES - 1, 1)
    logs = jax.random.uniform(key, (MODULES, FEAT), jnp.float32, jnp.log(0.1), jnp.log(10.0))
    return jnp.exp(logs) * 3.0 ** ramp


def touch_ends(values, key, smallest, high):
    longest = values.shape.index(max(values.shape))
    spots = []
    for shift in (0, 1):
        where = [jax.random.randint(jax.random.fold_in(key, axis), (), 0, length) for axis, length in enumerate(values.shape)]
        where[longest] = (where[longest] + shift) % values.shape[longest]
        spots.append(tuple(where))
    return values.at[spots[0]].set(smallest).at[spots[1]].set(high)


def steps_of(stream_key, shape, cuts, least, top_value):
    factor_of, own = 1.0, jax.random.fold_in(stream_key, 6)
    for axis_at, parts in cuts:
        steps = jnp.exp(jax.random.uniform(jax.random.fold_in(own, axis_at), (parts,), jnp.float32, least / len(cuts), top_value / len(cuts)))
        factor_of = factor_of * jnp.repeat(steps, shape[axis_at] // parts).reshape([-1 if axis == axis_at else 1 for axis in range(len(shape))])
    return factor_of


def centred(key, extent, spread, reach, pieces=(), kind=jnp.bfloat16):
    loudness = steps_of(key, extent, pieces, -0.22, 0.18) if pieces else 1.0
    result = jax.random.normal(key, extent, jnp.float32) * spread * loudness
    return jnp.minimum(jnp.maximum(result, -reach), reach).astype(kind)


def setup_inputs(seed: int = 0, part: int = 0) -> dict:
    seeds = jax.random.split(jax.random.key(seed), 8)
    part_splits = jax.random.split(jax.random.fold_in(seeds[7], part), 8)
    return {
        "query_pool": centred(part_splits[0], (QUERIES, MODULES, FEAT), 1.0, 6.0, ((1, 16),)),
        "train_store": centred(part_splits[1], (TRAIN, MODULES, FEAT), 1.0, 6.0, ((1, 16),)),
        "query_ids": touch_ends(jax.random.randint(part_splits[2], (QUERIES,), 0, QUERIES), jax.random.fold_in(part_splits[2], 1), 0, QUERIES - 1).astype(jnp.int32),
        "train_ids": touch_ends(jax.random.randint(part_splits[3], (TRAIN,), 0, TRAIN), jax.random.fold_in(part_splits[3], 1), 0, TRAIN - 1).astype(jnp.int32),
        "out_basis": centred(seeds[4], (MODULES, OUT, OUT), OUT ** -0.5, 0.75, ((0, 16),)),
        "in_basis": centred(seeds[5], (MODULES, IN, IN), IN ** -0.5, 0.75, ((0, 16),)),
        "eigenvalues": draw_eigenvalues(jax.random.fold_in(seeds[7], 71), part),
    }


def rotate(feat, outer, inner):
    grads = feat.astype(jnp.float32).reshape(feat.shape[0], OUT, IN)
    half = jnp.einsum('roi,ij->roj', grads, inner.astype(jnp.float32)).astype(jnp.bfloat16)
    rotated = jnp.einsum('op,roj->rpj', outer.astype(jnp.float32), half.astype(jnp.float32))
    return rotated.reshape(feat.shape[0], FEAT)

def reference(query_pool, train_store, query_ids, train_ids, out_basis, in_basis, eigenvalues):
    damp = 0.1 * jnp.mean(eigenvalues)

    def module_step(carry, index):
        total, self_term = carry
        queries = query_pool[query_ids, index]
        window = train_store[train_ids, index]
        denom = eigenvalues[index] + damp
        damped = (rotate(queries, out_basis[index], in_basis[index]) / denom[None, :]).astype(jnp.bfloat16)
        rotated_train = rotate(window, out_basis[index], in_basis[index]).astype(jnp.bfloat16)
        wide = rotated_train.astype(jnp.float32)
        self_term = self_term + lax.optimization_barrier(jnp.sum(wide * wide / denom[None, :], axis=1))
        total = total + jnp.dot(damped, rotated_train.T, preferred_element_type=jnp.float32)
        return ((total, self_term), None)
    start = (jnp.zeros((QUERIES, TRAIN), jnp.float32), jnp.zeros((TRAIN,), jnp.float32))
    (total, self_term), _ = lax.scan(module_step, start, jnp.arange(MODULES, dtype=jnp.int32))
    return total * lax.rsqrt(self_term)[None, :]
```

```python
import functools

import jax
import jax.numpy as jnp
from jax import lax
from jax.experimental import pallas as pl
from jax.experimental.pallas import tpu as pltpu
from jax.sharding import PartitionSpec as P

BF16 = jnp.bfloat16
F32 = jnp.float32
VMEM_LIMIT = 56 * 1024 * 1024
NN = (((1,), (0,)), ((), ()))
NT = (((1,), (1,)), ((), ()))


def dot(a, b, dims=NN):
    return lax.dot_general(a, b, dims, preferred_element_type=F32)


def iota(shape, dim):
    return lax.broadcasted_iota(jnp.int32, shape, dim)


def onehot(cond):
    return jnp.where(cond, 1.0, 0.0).astype(BF16)


def inner_weight(basis, side, pack):
    wide = side * pack
    rows = onehot(iota((wide, side), 0) // pack == iota((wide, side), 1))
    cols = onehot(iota((side, wide), 1) % side == iota((side, wide), 0))
    full = dot(dot(rows, basis, NT).astype(BF16), cols)
    keep = iota((wide, wide), 0) % pack == iota((wide, wide), 1) // side
    return jnp.where(keep, full, 0.0).astype(BF16)


def outer_weight(basis, side, pack):
    wide = side * pack
    rows = onehot(iota((wide, side), 0) % side == iota((wide, side), 1))
    k = iota((side, wide), 1)
    cols = onehot(k // (pack * pack) * pack + k % pack == iota((side, wide), 0))
    full = dot(dot(rows, basis, NT).astype(BF16), cols)
    keep = iota((wide, wide), 0) // side == iota((wide, wide), 1) // pack % pack
    return jnp.where(keep, full, 0.0).astype(BF16)


def outer_weight_t(basis, side, pack):
    wide = side * pack
    k = iota((wide, side), 0)
    rows = onehot(k // (pack * pack) * pack + k % pack == iota((wide, side), 1))
    cols = onehot(iota((side, wide), 1) % side == iota((side, wide), 0))
    full = dot(dot(rows, basis).astype(BF16), cols)
    keep = iota((wide, wide), 1) // side == iota((wide, wide), 0) // pack % pack
    return jnp.where(keep, full, 0.0).astype(BF16)


def halves(x_ref, weight, half_ref, side, pack):
    wide = side * pack
    groups = side // pack
    unit = pack * pack
    for g in range(groups):
        part = dot(weight, x_ref[:, g * wide : (g + 1) * wide], NT).astype(BF16)
        half_ref[:, g * unit : (g + 1) * unit, :] = part.reshape(groups, unit, part.shape[1])


def train_kernel(side, pack, x_ref, inner_ref, outer_ref, out_ref, half_ref, w3_ref, w4_ref):
    @pl.when(pl.program_id(0) == 0)
    def _():
        w3_ref[...] = inner_weight(inner_ref[...], side, pack)
        w4_ref[...] = outer_weight(outer_ref[...], side, pack)

    halves(x_ref, w3_ref[...], half_ref, side, pack)
    w4 = w4_ref[...]
    for g in range(side // pack):
        out_ref[g] = dot(w4, half_ref[g]).astype(BF16)


def query_kernel(side, pack, x_ref, inner_ref, out_ref, half_ref, w3_ref):
    @pl.when(pl.program_id(0) == 0)
    def _():
        w3_ref[...] = inner_weight(inner_ref[...], side, pack)

    halves(x_ref, w3_ref[...], half_ref, side, pack)
    for g in range(side // pack):
        out_ref[g] = half_ref[g].T


def rotate_train(x, inner, outer, block=256):
    rows, feat = x.shape
    side = inner.shape[0]
    pack = 256 // side
    groups, wide = side // pack, side * pack
    return pl.pallas_call(
        functools.partial(train_kernel, side, pack),
        out_shape=jax.ShapeDtypeStruct((groups, wide, rows), BF16),
        grid=(rows // block,),
        in_specs=[
            pl.BlockSpec((block, feat), lambda i: (i, 0)),
            pl.BlockSpec((side, side), lambda i: (0, 0)),
            pl.BlockSpec((side, side), lambda i: (0, 0)),
        ],
        out_specs=pl.BlockSpec((groups, wide, block), lambda i: (0, 0, i)),
        scratch_shapes=[
            pltpu.VMEM((groups, wide, block), BF16),
            pltpu.VMEM((wide, wide), BF16),
            pltpu.VMEM((wide, wide), BF16),
        ],
        compiler_params=pltpu.CompilerParams(vmem_limit_bytes=VMEM_LIMIT),
        cost_estimate=pl.CostEstimate(
            flops=4 * rows * feat * wide, bytes_accessed=4 * rows * feat, transcendentals=0
        ),
        name="rotate_train",
    )(x, inner, outer)


def rotate_query(x, inner, block=256):
    rows, feat = x.shape
    side = inner.shape[0]
    pack = 256 // side
    groups, wide = side // pack, side * pack
    return pl.pallas_call(
        functools.partial(query_kernel, side, pack),
        out_shape=jax.ShapeDtypeStruct((groups, rows, wide), BF16),
        grid=(rows // block,),
        in_specs=[
            pl.BlockSpec((block, feat), lambda i: (i, 0)),
            pl.BlockSpec((side, side), lambda i: (0, 0)),
        ],
        out_specs=pl.BlockSpec((groups, block, wide), lambda i: (0, i, 0)),
        scratch_shapes=[
            pltpu.VMEM((groups, wide, block), BF16),
            pltpu.VMEM((wide, wide), BF16),
        ],
        compiler_params=pltpu.CompilerParams(vmem_limit_bytes=VMEM_LIMIT),
        cost_estimate=pl.CostEstimate(
            flops=2 * rows * feat * wide, bytes_accessed=4 * rows * feat, transcendentals=0
        ),
        name="rotate_query",
    )(x, inner)


def row_ids_to_columns(ids_ref, start, length):
    pieces = [
        jnp.broadcast_to(ids_ref[:, start + s : start + s + 128], (128, 128)).T
        for s in range(0, length, 128)
    ]
    return pieces[0] if len(pieces) == 1 else jnp.concatenate(pieces, axis=0)


def score_kernel(
    side, pack, scale, rt_ref, hq_ref, eig_ref, sum_ref, outer_ref, ids_ref, out_ref, d_ref, p2_ref, oh_ref
):
    groups, wide, train = rt_ref.shape
    queries = hq_ref.shape[1]
    feat = groups * wide
    damp = sum_ref[0, 0] * scale
    inv = 1.0 / (eig_ref[...] + damp)
    w4t = outer_weight_t(outer_ref[...], side, pack)
    for s in range(0, train, 128):
        col = row_ids_to_columns(ids_ref, s, 128)
        for c in range(0, train, 128):
            hot = onehot(col == iota((128, 128), 1) + c)
            oh_ref[s : s + 128, c : c + 128] = hot
            oh_ref[s : s + 128, train + c : train + c + 128] = hot
    self_acc = [jnp.zeros((8, 128), F32) for _ in range(train // 128)]
    for g in range(groups):
        inv_g = inv[:, g * wide : (g + 1) * wide]
        d = dot(hq_ref[g], w4t) * inv_g
        d_ref[:, g * wide : (g + 1) * wide] = d.astype(BF16)
        col = jnp.broadcast_to(inv_g, (128, wide)).T
        for t in range(train // 128):
            r = rt_ref[g, :, t * 128 : (t + 1) * 128].astype(F32)
            self_acc[t] = self_acc[t] + (r * r * col).reshape(wide // 8, 8, 128).sum(0)
    self_row = jnp.concatenate([a.sum(0, keepdims=True) for a in self_acc], axis=1)
    rt = rt_ref[...].reshape(feat, train)
    for t in range(0, train, 256):
        p = dot(d_ref[...], rt[:, t : t + 256])
        hi = p.astype(BF16)
        p2_ref[:, t : t + 256] = hi
        p2_ref[:, train + t : train + t + 256] = (p - hi.astype(F32)).astype(BF16)
    half = train // 2
    for q in range(0, queries, 256):
        for part in range(2):
            base = part * (half + 8)
            out_ref[base : base + half, q : q + 256] = dot(
                oh_ref[part * half : (part + 1) * half, :], p2_ref[q : q + 256, :], NT
            )
    lines = train // queries
    tail = jnp.concatenate(
        [self_row[:, i * queries : (i + 1) * queries] for i in range(lines)]
        + [jnp.zeros((8 - lines, queries), F32)],
        axis=0,
    )
    for part in range(2):
        base = part * (half + 8) + half
        out_ref[base : base + 8, :] = tail


def partial_scores(rt, hq, eig, eig_sum, outer, ids, scale):
    groups, wide, train = rt.shape
    queries = hq.shape[1]
    side = outer.shape[0]
    whole = pl.BlockSpec(memory_space=pltpu.VMEM)
    return pl.pallas_call(
        functools.partial(score_kernel, side, 256 // side, scale),
        out_shape=jax.ShapeDtypeStruct((train + 16, queries), F32),
        in_specs=[whole, whole, whole, pl.BlockSpec(memory_space=pltpu.SMEM), whole, whole],
        out_specs=whole,
        scratch_shapes=[
            pltpu.VMEM((queries, groups * wide), BF16),
            pltpu.VMEM((queries, 2 * train), BF16),
            pltpu.VMEM((train, 2 * train), BF16),
        ],
        compiler_params=pltpu.CompilerParams(vmem_limit_bytes=VMEM_LIMIT),
        cost_estimate=pl.CostEstimate(
            flops=2 * queries * train * (groups * wide + 2 * train),
            bytes_accessed=2 * groups * wide * (train + queries) + 4 * train * queries,
            transcendentals=0,
        ),
        name="partial_scores",
    )(rt, hq, eig, eig_sum, outer, ids)


def split3(x):
    a = x.astype(BF16)
    rest = x - a.astype(F32)
    b = rest.astype(BF16)
    return a, b, (rest - b.astype(F32)).astype(BF16)


def final_kernel(train, mine_ref, got_ref, qids_ref, tids_ref, out_ref):
    columns, queries = out_ref.shape
    total = mine_ref[:columns, :] + got_ref[:columns, :]
    self_lines = mine_ref[columns:, :] + got_ref[columns:, :]
    lines = train // queries
    self_row = jnp.concatenate([self_lines[i : i + 1, :] for i in range(lines)], axis=1)
    ids = tids_ref[...]
    pick = jnp.where(ids == iota((columns, train), 1), self_row, 0.0)
    own = pick.sum(1, keepdims=True)
    scaled = total * lax.rsqrt(own)
    hot = onehot(iota((queries, queries), 0) == qids_ref[...])
    out_ref[...] = functools.reduce(lambda a, b: a + b, [dot(s, hot) for s in split3(scaled)])


def finish(mine, got, query_ids, train_ids, columns, train):
    queries = mine.shape[1]
    whole = pl.BlockSpec(memory_space=pltpu.VMEM)
    return pl.pallas_call(
        functools.partial(final_kernel, train),
        out_shape=jax.ShapeDtypeStruct((columns, queries), F32),
        in_specs=[whole] * 4,
        out_specs=whole,
        compiler_params=pltpu.CompilerParams(vmem_limit_bytes=VMEM_LIMIT),
        name="finish",
    )(mine, got, query_ids, train_ids)


def exchange(x, bit, devices):
    return lax.ppermute(x, "layer", [(i, i ^ bit) for i in range(devices)])


def shards(query_pool, train_store, query_ids, train_ids, out_basis, in_basis, eigenvalues):
    devices = lax.axis_size("layer")
    bits = devices.bit_length() - 1
    me = lax.axis_index("layer")
    train = train_store.shape[0]
    queries = query_pool.shape[0]
    side = out_basis.shape[1]
    columns = train // devices
    inner, outer = in_basis[0], out_basis[0]

    eig_sum = jnp.sum(eigenvalues).reshape(1, 1)
    for b in range(bits):
        eig_sum = eig_sum + exchange(eig_sum, 1 << b, devices)
    scale = 0.1 / (eigenvalues.shape[1] * devices)
    eig = eigenvalues.reshape(side, side).T.reshape(1, side * side)

    order = [sum(((k >> (bits - 1 - b)) & 1) << b for b in range(bits)) for k in range(devices)]
    blocks = train_ids.reshape(devices, columns)
    ids = jnp.stack([lax.dynamic_index_in_dim(blocks, me ^ k, 0, False) for k in order]).reshape(1, train)

    rt = rotate_train(train_store.reshape(train, -1), inner, outer)
    hq = rotate_query(query_pool.reshape(queries, -1), inner)
    both = partial_scores(rt, hq, eig, eig_sum, outer, ids, scale)

    rows = train // 2
    mine, sent = both[: rows + 8], both[rows + 8 :]
    for b in range(bits):
        got = exchange(sent, 1 << b, devices)
        if b < bits - 1:
            summed = mine + got
            rows //= 2
            mine, sent = jnp.concatenate([summed[:rows], summed[2 * rows :]]), summed[rows:]
    own_ids = lax.dynamic_index_in_dim(blocks, me, 0, False).reshape(columns, 1)
    out = finish(mine, got, query_ids.reshape(1, queries), own_ids, columns, train)
    return out.T


def solution(mesh):
    placed = (
        P("grp", "layer", None),
        P("grp", "layer", None),
        P("grp"),
        P("grp"),
        P("layer", None, None),
        P("layer", None, None),
        P("layer", None),
    )
    return jax.shard_map(
        shards, mesh=mesh, in_specs=placed, out_specs=P("grp", "layer"), check_vma=False
    )
```

```python
import functools

import jax
import jax.numpy as jnp
from jax import lax
from jax.experimental import pallas as pl
from jax.experimental.pallas import tpu as pltpu
from jax.sharding import PartitionSpec as P

BF16 = jnp.bfloat16
F32 = jnp.float32
VMEM_LIMIT = 56 * 1024 * 1024
CHUNKS = 2
NN = (((1,), (0,)), ((), ()))
NT = (((1,), (1,)), ((), ()))


def dot(a, b, dims=NN):
    return lax.dot_general(a, b, dims, preferred_element_type=F32)


def iota(shape, dim):
    return lax.broadcasted_iota(jnp.int32, shape, dim)


def onehot(cond):
    return jnp.where(cond, 1.0, 0.0).astype(BF16)


def even_first(place, side):
    return place % (side // 2) * 2 + place // (side // 2)


def inner_weight(basis, side, pack):
    wide = side * pack
    rows = onehot(iota((wide, side), 0) // pack == iota((wide, side), 1))
    cols = onehot(iota((side, wide), 1) % side == iota((side, wide), 0))
    full = dot(dot(rows, basis, NT).astype(BF16), cols)
    keep = iota((wide, wide), 0) % pack == iota((wide, wide), 1) // side
    return jnp.where(keep, full, 0.0).astype(BF16)


def outer_weight(basis, side, pack):
    wide = side * pack
    rows = onehot(even_first(iota((wide, side), 0) % side, side) == iota((wide, side), 1))
    k = iota((side, wide), 1)
    cols = onehot(k // (pack * pack) * pack + k % pack == iota((side, wide), 0))
    full = dot(dot(rows, basis, NT).astype(BF16), cols)
    keep = iota((wide, wide), 0) // side == iota((wide, wide), 1) // pack % pack
    return jnp.where(keep, full, 0.0).astype(BF16)


def outer_weight_t(basis, side, pack):
    wide = side * pack
    k = iota((wide, side), 0)
    rows = onehot(k // (pack * pack) * pack + k % pack == iota((wide, side), 1))
    cols = onehot(even_first(iota((side, wide), 1) % side, side) == iota((side, wide), 0))
    full = dot(dot(rows, basis).astype(BF16), cols)
    keep = iota((wide, wide), 1) // side == iota((wide, wide), 0) // pack % pack
    return jnp.where(keep, full, 0.0).astype(BF16)


def halves(x_ref, weight, half_ref, side, pack):
    wide = side * pack
    groups = side // pack
    unit = pack * pack
    for g in range(groups):
        part = dot(weight, x_ref[:, g * wide : (g + 1) * wide], NT).astype(BF16)
        half_ref[:, g * unit : (g + 1) * unit, :] = part.reshape(groups, unit, part.shape[1])


def in_vmem(x):
    return pltpu.with_memory_space_constraint(x, pltpu.VMEM)


WHOLE = pl.BlockSpec(memory_space=pltpu.VMEM)
IN_HBM = pl.BlockSpec(memory_space=pltpu.HBM)
ANYWHERE = pl.BlockSpec(memory_space=pl.ANY)


def kernel_call(body, name, args, outs, scratch=(), specs=None, flops=0, limit=VMEM_LIMIT):
    specs = specs or [WHOLE] * len(args)
    place = {id(IN_HBM): pltpu.HBM, id(WHOLE): pltpu.VMEM}
    args = [
        pltpu.with_memory_space_constraint(a, place[id(s)]) if id(s) in place and a.size > 2048 or s is IN_HBM else a
        for a, s in zip(args, specs)
    ]
    return pl.pallas_call(
        body,
        out_shape=tuple(pltpu.VMEM(shape, dtype) for shape, dtype in outs),
        in_specs=specs,
        out_specs=tuple([WHOLE] * len(outs)),
        scratch_shapes=list(scratch),
        compiler_params=pltpu.CompilerParams(vmem_limit_bytes=limit),
        cost_estimate=pl.CostEstimate(flops=flops, bytes_accessed=0, transcendentals=0),
        name=name,
    )(*args)


def fetch(pairs, sems):
    copies = [pltpu.make_async_copy(src, dst, sems.at[i]) for i, (src, dst) in enumerate(pairs)]
    for copy in copies:
        copy.start()
    return copies


def prepare_kernel(devices, side, pack, *refs):
    _, tids_any, qids_any, eig_any, inner_any, outer_any, x_any = refs[:7]
    sel_t_ref, sel_q_ref, eig_t_ref, w3_ref, w4_ref, w4t_ref, x_ref = refs[7:14]
    tids_ref, qids_ref, eig_ref, inner_ref, outer_ref, sems = refs[14:]
    small = ((tids_any, tids_ref), (qids_any, qids_ref), (eig_any, eig_ref), (inner_any, inner_ref), (outer_any, outer_ref))
    copies = fetch(small + ((x_any, x_ref),), sems)
    for copy in copies[:-1]:
        copy.wait()
    me = lax.axis_index("layer")
    train, queries = sel_t_ref.shape[0], sel_q_ref.shape[0]
    ids = jnp.broadcast_to(tids_ref[...], (8, train))
    lane = iota((8, train), 1)
    step = train // devices
    core = me % 2
    while step < train:
        bit = (lane // step) % 2
        other = jnp.where(bit == 0, pltpu.roll(ids, train - step, 1), pltpu.roll(ids, step, 1))
        ids = jnp.where(me % 2 == 1, other, ids)
        me = me // 2
        step *= 2
    owner = (core + lane // (train // devices)) % 2
    step = 2 * (train // devices)
    low, high = (lane // step) % 2, (lane // (2 * step)) % 2
    other = jnp.where(low > high, pltpu.roll(ids, train - step, 1), jnp.where(low < high, pltpu.roll(ids, step, 1), ids))
    ids = jnp.where(owner == 1, other, ids)
    for s in range(0, train, 128):
        col = jnp.broadcast_to(ids[0:1, s : s + 128], (128, 128)).T
        for c in range(0, train, 128):
            sel_t_ref[s : s + 128, c : c + 128] = onehot(col == iota((128, 128), 1) + c)
    sel_q_ref[...] = onehot(iota((queries, queries), 0) == qids_ref[...])
    eig = jnp.concatenate([eig_ref[:, c : c + 2 * side] for c in range(0, side * side, 2 * side)], axis=0)
    eig = eig.T
    eig = jnp.concatenate([eig[:side], eig[side:]], axis=1)
    for j in range(side):
        eig_t_ref[:, j * side : (j + 1) * side] = eig[j : j + 1, :]
    w3_ref[...] = inner_weight(inner_ref[...], side, pack)
    w4_ref[...] = outer_weight(outer_ref[...], side, pack)
    w4t_ref[...] = outer_weight_t(outer_ref[...], side, pack)
    copies[-1].wait()


def prepare(after, tids, qids, eig, inner, outer, x, devices):
    train, queries, side = tids.shape[1], qids.shape[1], inner.shape[0]
    pack = 256 // side
    wide = side * pack
    return kernel_call(
        functools.partial(prepare_kernel, devices, side, pack),
        "prepare",
        (after, tids, qids, eig, inner, outer, x),
        [((train, train), BF16), ((queries, queries), BF16), (eig.shape, F32)]
        + [((wide, wide), BF16)] * 3
        + [(x.shape, BF16)],
        [pltpu.VMEM(a.shape, a.dtype) for a in (tids, qids, eig, inner, outer)] + [pltpu.SemaphoreType.DMA((6,))],
        [ANYWHERE] + [IN_HBM] * 6,
        limit=6 << 20,
    )


def query_kernel(side, after_ref, x_ref, w3_ref, next_any, out_ref, next_ref, half_ref, sems):
    copies = fetch(((next_any.at[: next_ref.shape[0]], next_ref),), sems)
    pack = w3_ref.shape[0] // side
    halves(x_ref, w3_ref[...], half_ref, side, pack)
    for g in range(side // pack):
        out_ref[g] = half_ref[g].T
    copies[0].wait()


def rotate_query(after, x, w3, upcoming, rows_next, side):
    rows, feat = x.shape
    wide = w3.shape[0]
    groups = feat // wide
    return kernel_call(
        functools.partial(query_kernel, side),
        "rotate_query",
        (after, x, w3, upcoming),
        [((groups, rows, wide), BF16), ((rows_next, feat), BF16)],
        [pltpu.VMEM((groups, wide, rows), BF16), pltpu.SemaphoreType.DMA((1,))],
        [ANYWHERE, WHOLE, WHOLE, IN_HBM],
        flops=2 * rows * feat * wide,
        limit=12 << 20,
    )


def train_kernel(side, start, after_ref, x_ref, w3_ref, w4_ref, next_any, out_ref, *rest):
    half_ref, sems = rest[-2:]
    copies = []
    if start:
        (next_ref,) = rest[:-2]
        copies = fetch(((next_any.at[start : start + next_ref.shape[0]], next_ref),), sems)
    halves(x_ref, w3_ref[...], half_ref, side, w3_ref.shape[0] // side)
    w4 = w4_ref[...]
    for g in range(out_ref.shape[0]):
        out_ref[g] = dot(w4, half_ref[g]).astype(BF16)
    for copy in copies:
        copy.wait()


def rotate_train(after, x, w3, w4, upcoming, start, side):
    rows, feat = x.shape
    wide = w3.shape[0]
    groups = feat // wide
    outs = [((groups, wide, rows), BF16)]
    if start:
        outs.append(((rows, feat), BF16))
    return kernel_call(
        functools.partial(train_kernel, side, start),
        "rotate_train",
        (after, x, w3, w4, upcoming),
        outs,
        [pltpu.VMEM((groups, wide, rows), BF16), pltpu.SemaphoreType.DMA((1,))],
        [ANYWHERE, WHOLE, WHOLE, WHOLE, IN_HBM],
        flops=4 * rows * feat * wide,
        limit=12 << 20,
    )


def score_kernel(scale, devices, start, with_self, parts, *refs):
    refs = refs[1:]
    rt_refs = refs[:parts]
    hq_ref, eig_ref, sum_ref, w4t_ref, sel_ref, mine_ref, sent_ref, d_ref, p_ref = refs[parts:]
    groups, wide, cols = rt_refs[0].shape
    train = cols * parts
    queries = mine_ref.shape[1]
    feat = groups * wide
    inv = 1.0 / (eig_ref[...] + sum_ref[0:1, 0:1] * scale)
    w4t = w4t_ref[...]
    for g in range(groups):
        d = dot(hq_ref[g, start : start + queries, :], w4t) * inv[:, g * wide : (g + 1) * wide]
        d_ref[:, g * wide : (g + 1) * wide] = d.astype(BF16)
    for i, rt_ref in enumerate(rt_refs):
        rt = rt_ref[...].reshape(feat, cols)
        for t in range(0, cols, 256):
            p = dot(d_ref[...], rt[:, t : t + 256])
            hi = p.astype(BF16)
            at = i * cols + t
            p_ref[0, :, at : at + 256] = hi
            p_ref[1, :, at : at + 256] = (p - hi.astype(F32)).astype(BF16)
    half = train // 2
    columns = train // devices
    bits = devices.bit_length() - 1
    rows = min(half, 512)
    for base in range(0, train, rows):
        pick = sel_ref[base : base + rows, :]
        got = dot(pick, p_ref[0], NT) + dot(pick, p_ref[1], NT)
        for k in range(rows // columns):
            block = base // columns + k
            place = sum(((block >> i) & 1) << (bits - 1 - i) for i in range(bits))
            ref = (mine_ref, sent_ref)[place * columns // half]
            at = place * columns % half
            ref[at : at + columns, :] = got[k * columns : (k + 1) * columns, :]
    if with_self:
        sums = []
        for rt_ref in rt_refs:
            for t in range(0, cols, 128):
                acc = jnp.zeros((8, 128), F32)
                for g in range(groups):
                    col = jnp.broadcast_to(inv[:, g * wide : (g + 1) * wide], (128, wide)).T
                    r = rt_ref[g, :, t : t + 128].astype(F32)
                    acc = acc + (r * r * col).reshape(wide // 8, 8, 128).sum(0)
                sums.append(acc.sum(0, keepdims=True))
        per = queries // 128
        tail = [jnp.concatenate(sums[i : i + per], axis=1) for i in range(0, len(sums), per)]
        tail += [jnp.zeros((1, queries), F32)] * (8 - len(tail))
        tail = jnp.concatenate(tail, axis=0)
        mine_ref[half : half + 8, :] = tail
        sent_ref[half : half + 8, :] = tail


def partial_scores(after, rts, hq, eig, eig_sum, w4t, sel, scale, devices, start, queries, with_self):
    groups, wide, cols = rts[0].shape
    train = cols * len(rts)
    rows = train // 2 + 8 * with_self
    return kernel_call(
        functools.partial(score_kernel, scale, devices, start, with_self, len(rts)),
        "partial_scores",
        (after, *rts, hq, eig, eig_sum, w4t, sel),
        [((rows, queries), F32)] * 2,
        [pltpu.VMEM((queries, groups * wide), BF16), pltpu.VMEM((2, queries, train), BF16)],
        [ANYWHERE] + [WHOLE] * (len(rts) + 5),
        flops=2 * queries * train * (groups * wide + 2 * train),
        limit=16 << 20,
    )


def final_kernel(*refs):
    sel_t_ref, sel_ref, out_ref = refs[-3:]
    columns, queries = out_ref.shape
    train = sel_t_ref.shape[1]
    sums = [refs[i][...] + refs[i + 1][...] for i in range(0, len(refs) - 3, 2)]
    total = jnp.concatenate([s[:columns] for s in sums], axis=1)
    tail = sums[0][columns:]
    self_row = jnp.concatenate([tail[i : i + 1] for i in range(train // tail.shape[1])], axis=1)
    own = sel_t_ref[: max(columns, 16), :].astype(F32)[:columns]
    scaled = total * lax.rsqrt((own * self_row).sum(1, keepdims=True))
    hi = scaled.astype(BF16)
    rest = scaled - hi.astype(F32)
    mid = rest.astype(BF16)
    low = (rest - mid.astype(F32)).astype(BF16)
    sel = sel_ref[...]
    out_ref[...] = dot(hi, sel) + dot(mid, sel) + dot(low, sel)


def finish(pairs, sel_t, sel_q, columns):
    args = [a for pair in pairs for a in pair]
    return pl.pallas_call(
        final_kernel,
        out_shape=jax.ShapeDtypeStruct((columns, sel_q.shape[0]), F32),
        in_specs=[WHOLE] * (len(args) + 2),
        out_specs=WHOLE,
        compiler_params=pltpu.CompilerParams(vmem_limit_bytes=8 << 20),
        name="finish",
    )(*args, in_vmem(sel_t), in_vmem(sel_q))


def sum_kernel(x_ref, out_ref):
    out_ref[...] = jnp.broadcast_to(jnp.sum(x_ref[...], axis=1, keepdims=True), out_ref.shape)


def next_halves(mine, got, rows):
    total = mine + got
    rows //= 2
    return jnp.concatenate([total[:rows], total[2 * rows :]]), total[rows:]


def halving_step(x, step, devices):
    swap = {1: 2, 2: 1} if devices > 4 else {}
    pairs = [(i, i ^ (1 << (swap.get(step, step) if i % 2 else step))) for i in range(devices)]
    return lax.ppermute(x, "layer", pairs)


def exchange(x, bit, devices):
    return lax.ppermute(x, "layer", [(i, i ^ bit) for i in range(devices)])


def shards(query_pool, train_store, query_ids, train_ids, out_basis, in_basis, eigenvalues):
    devices = lax.axis_size("layer")
    bits = devices.bit_length() - 1
    train = train_store.shape[0]
    queries = query_pool.shape[0]
    side = out_basis.shape[1]
    columns = train // devices
    inner, outer = in_basis[0], out_basis[0]

    scale = 0.1 / (eigenvalues.shape[1] * devices)
    tids, qids = train_ids.reshape(1, train), query_ids.reshape(1, queries)
    xq, xt = query_pool.reshape(queries, -1), train_store.reshape(train, -1)

    half = train // 2
    eig_sum = kernel_call(sum_kernel, "eig_sum", (eigenvalues,), [((1, 128), F32)], limit=1 << 20)[0]
    for b in range(bits):
        got = exchange(eig_sum, 1 << b, devices)
        if b == 0:
            sel_t, sel_q, eig, w3, w4, w4t, xq = prepare(eig_sum, tids, qids, eigenvalues, inner, outer, xq, devices)
        elif b == 1:
            hq, xa = rotate_query(eig_sum, xq, w3, xt, half, side)
        elif b == 2:
            rta, xb = rotate_train(eig_sum, xa, w3, w4, xt, half, side)
        elif b == 3:
            (rtb,) = rotate_train(eig_sum, xb, w3, w4, xt, 0, side)
        eig_sum = eig_sum + got

    chunk = queries // CHUNKS
    after = eig_sum
    works = []
    for c in range(CHUNKS):
        mine, sent = partial_scores(
            after, (rta, rtb), hq, eig, eig_sum, w4t, sel_t, scale, devices, c * chunk, chunk, c == 0
        )
        mine, after = next_halves(mine, halving_step(sent, 0, devices), half)
        works.append((mine, after))
    pairs = []
    for mine, sent in works:
        for b in range(1, bits):
            got = halving_step(sent, b, devices)
            if b < bits - 1:
                mine, sent = next_halves(mine, got, half >> b)
        pairs.append((mine, got))
    return finish(pairs, sel_t, sel_q, columns).T


def solution(mesh):
    placed = (
        P("grp", "layer", None),
        P("grp", "layer", None),
        P("grp"),
        P("grp"),
        P("layer", None, None),
        P("layer", None, None),
        P("layer", None),
    )
    return jax.shard_map(
        shards, mesh=mesh, in_specs=placed, out_specs=P("grp", "layer"), check_vma=False
    )
```

```python
import functools

import jax
import jax.numpy as jnp
from jax import lax
from jax.experimental import pallas as pl
from jax.experimental.pallas import tpu as pltpu
from jax.sharding import PartitionSpec as P

BF16 = jnp.bfloat16
F32 = jnp.float32
VMEM_LIMIT = 56 * 1024 * 1024
NN = (((1,), (0,)), ((), ()))
NT = (((1,), (1,)), ((), ()))


def dot(a, b, dims=NN):
    return lax.dot_general(a, b, dims, preferred_element_type=F32)


def iota(shape, dim):
    return lax.broadcasted_iota(jnp.int32, shape, dim)


def onehot(cond):
    return jnp.where(cond, 1.0, 0.0).astype(BF16)


def even_first(place, side):
    return place % (side // 2) * 2 + place // (side // 2)


def inner_weight(basis, side, pack):
    wide = side * pack
    rows = onehot(iota((wide, side), 0) // pack == iota((wide, side), 1))
    cols = onehot(iota((side, wide), 1) % side == iota((side, wide), 0))
    full = dot(dot(rows, basis, NT).astype(BF16), cols)
    keep = iota((wide, wide), 0) % pack == iota((wide, wide), 1) // side
    return jnp.where(keep, full, 0.0).astype(BF16)


def outer_weight(basis, side, pack):
    wide = side * pack
    rows = onehot(even_first(iota((wide, side), 0) % side, side) == iota((wide, side), 1))
    k = iota((side, wide), 1)
    cols = onehot(k // (pack * pack) * pack + k % pack == iota((side, wide), 0))
    full = dot(dot(rows, basis, NT).astype(BF16), cols)
    keep = iota((wide, wide), 0) // side == iota((wide, wide), 1) // pack % pack
    return jnp.where(keep, full, 0.0).astype(BF16)


def outer_weight_t(basis, side, pack):
    wide = side * pack
    k = iota((wide, side), 0)
    rows = onehot(k // (pack * pack) * pack + k % pack == iota((wide, side), 1))
    cols = onehot(even_first(iota((side, wide), 1) % side, side) == iota((side, wide), 0))
    full = dot(dot(rows, basis).astype(BF16), cols)
    keep = iota((wide, wide), 1) // side == iota((wide, wide), 0) // pack % pack
    return jnp.where(keep, full, 0.0).astype(BF16)


def halves(x_ref, weight, half_ref, side, pack):
    wide = side * pack
    groups = side // pack
    unit = pack * pack
    for g in range(groups):
        part = dot(weight, x_ref[:, g * wide : (g + 1) * wide], NT).astype(BF16)
        half_ref[:, g * unit : (g + 1) * unit, :] = part.reshape(groups, unit, part.shape[1])


def in_vmem(x):
    return pltpu.with_memory_space_constraint(x, pltpu.VMEM)


WHOLE = pl.BlockSpec(memory_space=pltpu.VMEM)
IN_HBM = pl.BlockSpec(memory_space=pltpu.HBM)
ANYWHERE = pl.BlockSpec(memory_space=pl.ANY)


def kernel_call(body, name, args, outs, scratch=(), specs=None, flops=0, limit=VMEM_LIMIT, aliases=None):
    specs = specs or [WHOLE] * len(args)
    place = {id(IN_HBM): pltpu.HBM, id(WHOLE): pltpu.VMEM}
    args = [
        pltpu.with_memory_space_constraint(a, place[id(s)]) if id(s) in place and a.size > 2048 or s is IN_HBM else a
        for a, s in zip(args, specs)
    ]
    return pl.pallas_call(
        body,
        out_shape=tuple(pltpu.VMEM(shape, dtype) for shape, dtype in outs),
        in_specs=specs,
        out_specs=tuple([WHOLE] * len(outs)),
        scratch_shapes=list(scratch),
        input_output_aliases=aliases or {},
        compiler_params=pltpu.CompilerParams(vmem_limit_bytes=limit),
        cost_estimate=pl.CostEstimate(flops=flops, bytes_accessed=0, transcendentals=0),
        name=name,
    )(*args)


def fetch(pairs, sems):
    copies = [pltpu.make_async_copy(src, dst, sems.at[i]) for i, (src, dst) in enumerate(pairs)]
    for copy in copies:
        copy.start()
    return copies


def beside_fetch(compute):
    pl.when(lax.axis_index("layer") >= 0)(compute)


def rows_from(x_any, x_ref, start, stop):
    return x_any.at[start:stop], x_ref.at[start:stop]


def swap_bits(ids, low, high, columns, where=True):
    train = ids.shape[1]
    block = iota(ids.shape, 1) // columns
    a, b = (block >> low) & 1, (block >> high) & 1
    shift = ((1 << high) - (1 << low)) * columns
    up, down = pltpu.roll(ids, train - shift, 1), pltpu.roll(ids, shift, 1)
    return jnp.where((a > b) & where, up, jnp.where((a < b) & where, down, ids))


def prepare_kernel(devices, side, pack, have, *refs):
    tids_ref, qids_ref, eig_ref, inner_ref, outer_ref, x_any = refs[1:7]
    sel_t_ref, sel_q_ref, eig_t_ref, w3_ref, w4_ref, w4t_ref, x_ref = refs[8:15]
    copies = fetch((rows_from(x_any, x_ref, have, x_ref.shape[0]),), refs[15])
    @beside_fetch
    def _():
        me = lax.axis_index("layer")
        train, queries = sel_t_ref.shape[0], sel_q_ref.shape[0]
        ids = jnp.broadcast_to(tids_ref[...], (8, train))
        lane = iota((8, train), 1)
        step = train // devices
        core = me % 2
        while step < train:
            bit = (lane // step) % 2
            other = jnp.where(bit == 0, pltpu.roll(ids, train - step, 1), pltpu.roll(ids, step, 1))
            ids = jnp.where(me % 2 == 1, other, ids)
            me = me // 2
            step *= 2
        columns = train // devices
        bits = devices.bit_length() - 1
        if bits > 2:
            ids = swap_bits(ids, 1, 2, columns, (core + lane // columns) % 2 == 1)
        for b in range(bits // 2):
            ids = swap_bits(ids, b, bits - 1 - b, columns)
        for s in range(0, train, 128):
            col = jnp.broadcast_to(ids[0:1, s : s + 128], (128, 128)).T
            for c in range(0, train, 128):
                sel_t_ref[s : s + 128, c : c + 128] = onehot(col == iota((128, 128), 1) + c)
        sel_q_ref[...] = onehot(iota((queries, queries), 0) == qids_ref[...])
        eig = jnp.concatenate([eig_ref[:, c : c + 2 * side] for c in range(0, side * side, 2 * side)], axis=0)
        eig = eig.T
        eig = jnp.concatenate([eig[:side], eig[side:]], axis=1)
        for j in range(side):
            eig_t_ref[:, j * side : (j + 1) * side] = eig[j : j + 1, :]
        w3_ref[...] = inner_weight(inner_ref[...], side, pack)
        w4_ref[...] = outer_weight(outer_ref[...], side, pack)
        w4t_ref[...] = outer_weight_t(outer_ref[...], side, pack)

    copies[-1].wait()


def prepare(after, tids, qids, eig, inner, outer, x, part, have, devices):
    train, queries, side = tids.shape[1], qids.shape[1], inner.shape[0]
    pack = 256 // side
    wide = side * pack
    return kernel_call(
        functools.partial(prepare_kernel, devices, side, pack, have),
        "prepare",
        (after, tids, qids, eig, inner, outer, x, part),
        [((train, train), BF16), ((queries, queries), BF16), (eig.shape, F32)]
        + [((wide, wide), BF16)] * 3
        + [(x.shape, BF16)],
        [pltpu.SemaphoreType.DMA((1,))],
        [ANYWHERE] + [WHOLE] * 5 + [IN_HBM, WHOLE],
        limit=6 << 20,
        aliases={7: 6},
    )


def query_kernel(side, ahead, after_ref, x_ref, w3_ref, next_any, out_ref, next_ref, last_ref, half_ref, sems):
    rows = next_ref.shape[0]
    copies = fetch((rows_from(next_any, next_ref, 0, rows), (next_any.at[rows : rows + ahead], last_ref.at[:ahead])), sems)
    @beside_fetch
    def _():
        pack = w3_ref.shape[0] // side
        wide = w3_ref.shape[0]
        groups, unit = side // pack, pack * pack
        w3 = w3_ref[...]
        queries = x_ref.shape[0]
        block = min(queries, 256)
        for r in range(0, queries + block, block):
            for g in range(groups):
                if r < queries:
                    part = dot(w3, x_ref[r : r + block, g * wide : (g + 1) * wide], NT).astype(BF16)
                    half_ref[:, g * unit : (g + 1) * unit, r : r + block] = part.reshape(groups, unit, block)
                if r:
                    out_ref[g, r - block : r, :] = half_ref[g, :, r - block : r].T

    for copy in copies:
        copy.wait()


def rotate_query(after, x, w3, upcoming, rows_next, ahead, side):
    rows, feat = x.shape
    wide = w3.shape[0]
    groups = feat // wide
    return kernel_call(
        functools.partial(query_kernel, side, ahead),
        "rotate_query",
        (after, x, w3, upcoming),
        [((groups, rows, wide), BF16), ((rows_next, feat), BF16), ((rows_next, feat), BF16)],
        [pltpu.VMEM((groups, wide, rows), BF16), pltpu.SemaphoreType.DMA((2,))],
        [ANYWHERE, WHOLE, WHOLE, IN_HBM],
        flops=2 * rows * feat * wide,
        limit=12 << 20,
    )


def rotate_rows(side, x_ref, w3_ref, w4_ref, out_ref, half_ref):
    halves(x_ref, w3_ref[...], half_ref, side, w3_ref.shape[0] // side)
    w4 = w4_ref[...]
    for g in range(out_ref.shape[0]):
        out_ref[g] = dot(w4, half_ref[g]).astype(BF16)


def train_kernel(side, after_ref, x_ref, w3_ref, w4_ref, out_ref, half_ref):
    rotate_rows(side, x_ref, w3_ref, w4_ref, out_ref, half_ref)


def train_fetch_kernel(side, have, after_ref, x_ref, w3_ref, w4_ref, next_any, part_ref, out_ref, next_ref, half_ref, sems):
    rows = next_ref.shape[0]
    copies = fetch(((next_any.at[rows + have :], next_ref.at[have:]),), sems)

    @beside_fetch
    def _():
        rotate_rows(side, x_ref, w3_ref, w4_ref, out_ref, half_ref)

    copies[0].wait()


def rotate_train(after, x, w3, w4, side, upcoming=None, part=None, have=0):
    rows, feat = x.shape
    wide = w3.shape[0]
    groups = feat // wide
    body, args, sems, extra = functools.partial(train_kernel, side), (), [], {}
    outs = [((groups, wide, rows), BF16)]
    specs = [ANYWHERE, WHOLE, WHOLE, WHOLE]
    if upcoming is not None:
        body, args = functools.partial(train_fetch_kernel, side, have), (upcoming, part)
        outs.append(((rows, feat), BF16))
        sems = [pltpu.SemaphoreType.DMA((1,))]
        specs += [IN_HBM, WHOLE]
        extra = {"aliases": {5: 1}}
    return kernel_call(
        body,
        "rotate_train",
        (after, x, w3, w4, *args),
        outs,
        [pltpu.VMEM((groups, wide, rows), BF16)] + sems,
        specs,
        flops=4 * rows * feat * wide,
        limit=12 << 20,
        **extra,
    )


def damped_queries(d_ref, hq_ref, w4t_ref, inv, start):
    queries = d_ref.shape[0]
    groups, _, wide = hq_ref.shape
    w4t = w4t_ref[...]
    for g in range(groups):
        d = dot(hq_ref[g, start : start + queries, :], w4t) * inv[:, g * wide : (g + 1) * wide]
        d_ref[:, g * wide : (g + 1) * wide] = d.astype(BF16)


def multiply(p_ref, d_ref, rt_ref, at, inv_cols=()):
    groups, wide, cols = rt_ref.shape
    rt = rt_ref[...].reshape(groups * wide, cols)
    sums = []
    for t in range(0, cols, 256):
        p = dot(d_ref[...], rt[:, t : t + 256])
        if inv_cols:
            sums += self_sums(rt_ref, inv_cols, t, 256)
        hi = p.astype(BF16)
        p_ref[0, :, at + t : at + t + 256] = hi
        p_ref[1, :, at + t : at + t + 256] = (p - hi.astype(F32)).astype(BF16)
    return sums


def select_rows(p_refs, sel_ref, start, out_ref, rows):
    at, got = 0, None
    for p_ref in p_refs:
        cols = p_ref.shape[2]
        pick = sel_ref[start : start + rows, at : at + cols]
        for i in range(2):
            part = dot(pick, p_ref[i], NT)
            got = part if got is None else got + part
        at += cols
    out_ref[:rows, :] = got


def self_sums(rt_ref, inv_cols, at, cols):
    sums = []
    for t in range(at, at + cols, 128):
        acc = jnp.zeros((8, 128), F32)
        for g, col in enumerate(inv_cols):
            r = rt_ref[g, :, t : t + 128].astype(F32)
            acc = acc + (r * r * col[...]).reshape(-1, 8, 128).sum(0)
        sums.append(acc.sum(0, keepdims=True))
    return sums


def on_lines(sums, queries):
    per = queries // 128
    tail = [jnp.concatenate(sums[i : i + per], axis=1) for i in range(0, len(sums), per)]
    tail += [jnp.zeros((1, queries), F32)] * (8 - len(tail))
    return jnp.concatenate(tail, axis=0)


def score_kernel(scale, rta_ref, rtb_ref, hq_ref, eig_ref, sum_ref, w4t_ref, sel_ref, sent_ref, p_ref, tail_ref, d_ref, inv_ref):
    inv = 1.0 / (eig_ref[...] + sum_ref[0:1, 0:1] * scale)
    damped_queries(d_ref, hq_ref, w4t_ref, inv, 0)
    groups, wide, _ = rta_ref.shape
    for g in range(groups):
        inv_ref[g] = jnp.broadcast_to(inv[:, g * wide : (g + 1) * wide], (128, wide)).T
    inv_cols = [inv_ref.at[g] for g in range(groups)]
    sums = multiply(p_ref, d_ref, rta_ref, 0, inv_cols)
    sums += multiply(p_ref, d_ref, rtb_ref, rta_ref.shape[2], inv_cols)
    half = sel_ref.shape[0] // 2
    select_rows((p_ref,), sel_ref, half, sent_ref, half)
    tail = on_lines(sums, sent_ref.shape[1])
    sent_ref[half:, :] = tail
    tail_ref[...] = tail


def partial_scores(rts, hq, eig, eig_sum, w4t, sel, scale, queries):
    train = sel.shape[0]
    feat = eig.shape[1]
    return kernel_call(
        functools.partial(score_kernel, scale),
        "scores_self",
        (*rts, hq, eig, eig_sum, w4t, sel),
        [((train // 2 + 8, queries), F32), ((2, queries, train), BF16), ((8, queries), F32)],
        [pltpu.VMEM((queries, feat), BF16), pltpu.VMEM((*rts[0].shape[:2], 128), F32)],
        limit=16 << 20,
    )


def score_first_kernel(scale, start, after_ref, rt_ref, hq_ref, eig_ref, sum_ref, w4t_ref, d_ref, p_ref):
    inv = 1.0 / (eig_ref[...] + sum_ref[0:1, 0:1] * scale)
    damped_queries(d_ref, hq_ref, w4t_ref, inv, start)
    multiply(p_ref, d_ref, rt_ref, 0)


def score_first(after, rt, hq, eig, eig_sum, w4t, scale, start, queries):
    feat, cols = eig.shape[1], rt.shape[2]
    return kernel_call(
        functools.partial(score_first_kernel, scale, start),
        "scores_first",
        (after, rt, hq, eig, eig_sum, w4t),
        [((queries, feat), BF16), ((2, queries, cols), BF16)],
        (),
        [ANYWHERE] + [WHOLE] * 5,
        limit=8 << 20,
    )


def score_second_kernel(after_ref, rt_ref, d_ref, pa_ref, sel_ref, sent_ref, p_ref):
    multiply(p_ref, d_ref, rt_ref, 0)
    half = sel_ref.shape[0] // 2
    select_rows((pa_ref, p_ref), sel_ref, half, sent_ref, half)


def score_second(after, rt, d, pa, sel):
    queries = d.shape[0]
    train, cols = sel.shape[0], rt.shape[2]
    return kernel_call(
        score_second_kernel,
        "scores_second",
        (after, rt, d, pa, sel),
        [((train // 2, queries), F32), ((2, queries, cols), BF16)],
        (),
        [ANYWHERE] + [WHOLE] * 4,
        limit=8 << 20,
    )


def keep_kernel(parts, *refs):
    sel_ref, out_ref = refs[parts + 1], refs[-1]
    half = sel_ref.shape[0] // 2
    select_rows(refs[1 : parts + 1], sel_ref, 0, out_ref, half)
    if len(refs) > parts + 3:
        out_ref[half:, :] = refs[parts + 2][...]


def keep_rows(after, ps, sel, tail=None):
    queries = ps[0].shape[1]
    args = (after, *ps, sel) + (() if tail is None else (tail,))
    return kernel_call(
        functools.partial(keep_kernel, len(ps)),
        "keep_rows",
        args,
        [((sel.shape[0] // 2 + (0 if tail is None else 8), queries), F32)],
        (),
        [ANYWHERE] + [WHOLE] * (len(args) - 1),
        limit=8 << 20,
    )[0]


def pick_queries(scaled, sel):
    hi = scaled.astype(BF16)
    rest = scaled - hi.astype(F32)
    mid = rest.astype(BF16)
    low = (rest - mid.astype(F32)).astype(BF16)
    return dot(hi, sel) + dot(mid, sel) + dot(low, sel)


def finish_first_kernel(mine_ref, got_ref, sel_t_ref, sel_q_ref, out_ref, norm_ref):
    columns = out_ref.shape[0]
    width = mine_ref.shape[1]
    total = mine_ref[...] + got_ref[...]
    train = sel_t_ref.shape[1]
    self_row = jnp.concatenate([total[columns + i : columns + i + 1] for i in range(train // width)], axis=1)
    own = sel_t_ref[: max(columns, 16), :].astype(F32)[:columns]
    norm = lax.rsqrt((own * self_row).sum(1, keepdims=True))
    norm_ref[...] = jnp.broadcast_to(norm, norm_ref.shape)
    out_ref[...] = pick_queries(total[:columns] * norm, sel_q_ref[:width, :])


def finish_second_kernel(mine_ref, got_ref, first_ref, norm_ref, sel_q_ref, out_ref):
    width = mine_ref.shape[1]
    total = (mine_ref[...] + got_ref[...]) * norm_ref[:, 0:1]
    out_ref[...] = first_ref[...] + pick_queries(total, sel_q_ref[sel_q_ref.shape[0] - width :, :])


def finish(first, second, sel_t, sel_q, columns):
    queries = sel_q.shape[0]
    out, norm = kernel_call(
        finish_first_kernel,
        "finish_first",
        (*first, sel_t, sel_q),
        [((columns, queries), F32), ((columns, 128), F32)],
        limit=4 << 20,
    )
    args = [in_vmem(a) for a in (*second, out, norm, sel_q)]
    return pl.pallas_call(
        finish_second_kernel,
        out_shape=jax.ShapeDtypeStruct((columns, queries), F32),
        in_specs=[WHOLE] * len(args),
        out_specs=WHOLE,
        compiler_params=pltpu.CompilerParams(vmem_limit_bytes=4 << 20),
        name="finish_second",
    )(*args)


def sum_kernel(ahead, count, *refs):
    smalls, x_any, out_ref, held, part_ref, sems = refs[:count], refs[count], refs[count + 1], refs[count + 2 : -2], refs[-2], refs[-1]
    copies = fetch((*zip(smalls, held), rows_from(x_any, part_ref, 0, ahead)), sems)
    copies[0].wait()
    x_ref = held[0]
    out_ref[...] = jnp.broadcast_to(jnp.sum(x_ref[...], axis=1, keepdims=True), out_ref.shape)
    for copy in copies[1:]:
        copy.wait()


def next_halves(mine, got, rows):
    total = mine + got
    rows //= 2
    return jnp.concatenate([total[:rows], total[2 * rows :]]), total[rows:]


def halving_step(x, step, devices):
    swap = {1: 2, 2: 1} if devices > 4 else {}
    pairs = [(i, i ^ (1 << (swap.get(step, step) if i % 2 else step))) for i in range(devices)]
    return lax.ppermute(x, "layer", pairs)


def exchange(x, bit, devices):
    return lax.ppermute(x, "layer", [(i, i ^ bit) for i in range(devices)])


def shards(query_pool, train_store, query_ids, train_ids, out_basis, in_basis, eigenvalues):
    devices = lax.axis_size("layer")
    bits = devices.bit_length() - 1
    train = train_store.shape[0]
    queries = query_pool.shape[0]
    side = out_basis.shape[1]
    columns = train // devices
    inner, outer = in_basis[0], out_basis[0]

    scale = 0.1 / (eigenvalues.shape[1] * devices)
    tids, qids = train_ids.reshape(1, train), query_ids.reshape(1, queries)
    xq, xt = query_pool.reshape(queries, -1), train_store.reshape(train, -1)

    half = train // 2
    have_q, have_b = 128, 64
    smalls = (eigenvalues, tids, qids, inner, outer)
    eig_sum, eig_v, tids_v, qids_v, inner_v, outer_v, xq_part = kernel_call(
        functools.partial(sum_kernel, have_q, len(smalls)),
        "eig_sum",
        (*smalls, xq),
        [((1, 128), F32)] + [(a.shape, a.dtype) for a in smalls] + [(xq.shape, BF16)],
        [pltpu.SemaphoreType.DMA((6,))],
        [IN_HBM] * 6,
        limit=1 << 20,
    )
    for b in range(bits):
        got = exchange(eig_sum, 1 << b, devices)
        if b == 0:
            sel_t, sel_q, eig, w3, w4, w4t, xq = prepare(
                eig_sum, tids_v, qids_v, eig_v, inner_v, outer_v, xq, xq_part, have_q, devices
            )
        elif b == 1:
            hq, xa, xb = rotate_query(eig_sum, xq, w3, xt, half, have_b, side)
        elif b == 2:
            rta, xb = rotate_train(eig_sum, xa, w3, w4, side, xt, xb, have_b)
        elif b == 3:
            (rtb,) = rotate_train(eig_sum, xb, w3, w4, side)
        eig_sum = eig_sum + got

    chunk = queries // 2
    sent_a, p_a, tail = partial_scores((rta, rtb), hq, eig, eig_sum, w4t, sel_t, scale, chunk)
    got_a = halving_step(sent_a, 0, devices)
    mine_a = keep_rows(sent_a, [p_a], sel_t, tail)
    d, p_b1 = score_first(sent_a, rta, hq, eig, eig_sum, w4t, scale, chunk, chunk)
    mine_a, sent_a = next_halves(mine_a, got_a, half)
    sent_b, p_b2 = score_second(sent_a, rtb, d, p_b1, sel_t)
    got_b = halving_step(sent_b, 0, devices)
    mine_b = keep_rows(sent_b, [p_b1, p_b2], sel_t)
    got_a = halving_step(sent_a, 1, devices)
    pairs = [(mine_a, got_a), (mine_b, got_b)]
    for b in range(1, bits):
        for c in range(2):
            step = b + 1 - c
            if step < bits:
                mine, sent = next_halves(*pairs[c], half >> (step - 1))
                pairs[c] = (mine, halving_step(sent, step, devices))
    return finish(*pairs, sel_t, sel_q, columns).T


def solution(mesh):
    placed = (
        P("grp", "layer", None),
        P("grp", "layer", None),
        P("grp"),
        P("grp"),
        P("layer", None, None),
        P("layer", None, None),
        P("layer", None),
    )
    return jax.shard_map(
        shards, mesh=mesh, in_specs=placed, out_specs=P("grp", "layer"), check_vma=False
    )
```

```python
import functools

import jax
import jax.numpy as jnp
from jax import lax
from jax.experimental import pallas as pl
from jax.experimental.pallas import tpu as pltpu
from jax.sharding import PartitionSpec as P

BF16 = jnp.bfloat16
F32 = jnp.float32
VMEM_LIMIT = 56 * 1024 * 1024
NN = (((1,), (0,)), ((), ()))
NT = (((1,), (1,)), ((), ()))


def dot(a, b, dims=NN):
    return lax.dot_general(a, b, dims, preferred_element_type=F32)


def iota(shape, dim):
    return lax.broadcasted_iota(jnp.int32, shape, dim)


def onehot(cond):
    return jnp.where(cond, 1.0, 0.0).astype(BF16)


def even_first(place, side):
    return place % (side // 2) * 2 + place // (side // 2)


def inner_weight(basis, side, pack):
    wide = side * pack
    rows = onehot(iota((wide, side), 0) // pack == iota((wide, side), 1))
    cols = onehot(iota((side, wide), 1) % side == iota((side, wide), 0))
    full = dot(dot(rows, basis, NT).astype(BF16), cols)
    keep = iota((wide, wide), 0) % pack == iota((wide, wide), 1) // side
    return jnp.where(keep, full, 0.0).astype(BF16)


def outer_weight(basis, side, pack):
    wide = side * pack
    rows = onehot(even_first(iota((wide, side), 0) % side, side) == iota((wide, side), 1))
    k = iota((side, wide), 1)
    cols = onehot(k // (pack * pack) * pack + k % pack == iota((side, wide), 0))
    full = dot(dot(rows, basis, NT).astype(BF16), cols)
    keep = iota((wide, wide), 0) // side == iota((wide, wide), 1) // pack % pack
    return jnp.where(keep, full, 0.0).astype(BF16)


def outer_weight_t(basis, side, pack):
    wide = side * pack
    k = iota((wide, side), 0)
    rows = onehot(k // (pack * pack) * pack + k % pack == iota((wide, side), 1))
    cols = onehot(even_first(iota((side, wide), 1) % side, side) == iota((side, wide), 0))
    full = dot(dot(rows, basis).astype(BF16), cols)
    keep = iota((wide, wide), 1) // side == iota((wide, wide), 0) // pack % pack
    return jnp.where(keep, full, 0.0).astype(BF16)


def halves(x_ref, weight, half_ref, side, pack):
    wide = side * pack
    groups = side // pack
    unit = pack * pack
    for g in range(groups):
        part = dot(weight, x_ref[:, g * wide : (g + 1) * wide], NT).astype(BF16)
        half_ref[:, g * unit : (g + 1) * unit, :] = part.reshape(groups, unit, part.shape[1])


def in_vmem(x):
    return pltpu.with_memory_space_constraint(x, pltpu.VMEM)


WHOLE = pl.BlockSpec(memory_space=pltpu.VMEM)
IN_HBM = pl.BlockSpec(memory_space=pltpu.HBM)
ANYWHERE = pl.BlockSpec(memory_space=pl.ANY)


def kernel_call(body, name, args, outs, scratch=(), specs=None, flops=0, limit=VMEM_LIMIT, aliases=None):
    specs = specs or [WHOLE] * len(args)
    place = {id(IN_HBM): pltpu.HBM, id(WHOLE): pltpu.VMEM}
    args = [
        pltpu.with_memory_space_constraint(a, place[id(s)]) if id(s) in place and a.size > 2048 or s is IN_HBM else a
        for a, s in zip(args, specs)
    ]
    return pl.pallas_call(
        body,
        out_shape=tuple(pltpu.VMEM(shape, dtype) for shape, dtype in outs),
        in_specs=specs,
        out_specs=tuple([WHOLE] * len(outs)),
        scratch_shapes=list(scratch),
        input_output_aliases=aliases or {},
        compiler_params=pltpu.CompilerParams(vmem_limit_bytes=limit),
        cost_estimate=pl.CostEstimate(flops=flops, bytes_accessed=0, transcendentals=0),
        name=name,
    )(*args)


def fetch(pairs, sems):
    copies = [pltpu.make_async_copy(src, dst, sems.at[i]) for i, (src, dst) in enumerate(pairs)]
    for copy in copies:
        copy.start()
    return copies


def beside_fetch(compute):
    pl.when(lax.axis_index("layer") >= 0)(compute)


def rows_from(x_any, x_ref, start, stop):
    return x_any.at[start:stop], x_ref.at[start:stop]


def swap_bits(ids, low, high, columns, where=True):
    train = ids.shape[1]
    block = iota(ids.shape, 1) // columns
    a, b = (block >> low) & 1, (block >> high) & 1
    shift = ((1 << high) - (1 << low)) * columns
    up, down = pltpu.roll(ids, train - shift, 1), pltpu.roll(ids, shift, 1)
    return jnp.where((a > b) & where, up, jnp.where((a < b) & where, down, ids))


def prepare_kernel(devices, side, pack, have, *refs):
    tids_ref, qids_ref, eig_ref, inner_ref, outer_ref, x_any = refs[1:7]
    sel_t_ref, sel_q_ref, eig_t_ref, w3_ref, w4_ref, w4t_ref, x_ref = refs[8:15]
    copies = fetch((rows_from(x_any, x_ref, have, x_ref.shape[0]),), refs[15])
    @beside_fetch
    def _():
        me = lax.axis_index("layer")
        train, queries = sel_t_ref.shape[0], sel_q_ref.shape[0]
        ids = jnp.broadcast_to(tids_ref[...], (8, train))
        lane = iota((8, train), 1)
        step = train // devices
        core = me % 2
        while step < train:
            bit = (lane // step) % 2
            other = jnp.where(bit == 0, pltpu.roll(ids, train - step, 1), pltpu.roll(ids, step, 1))
            ids = jnp.where(me % 2 == 1, other, ids)
            me = me // 2
            step *= 2
        columns = train // devices
        bits = devices.bit_length() - 1
        if bits > 2:
            ids = swap_bits(ids, 1, 2, columns, (core + lane // columns) % 2 == 1)
        for b in range(bits // 2):
            ids = swap_bits(ids, b, bits - 1 - b, columns)
        for s in range(0, train, 128):
            col = jnp.broadcast_to(ids[0:1, s : s + 128], (128, 128)).T
            for c in range(0, train, 128):
                sel_t_ref[s : s + 128, c : c + 128] = onehot(col == iota((128, 128), 1) + c)
        sel_q_ref[...] = onehot(iota((queries, queries), 0) == qids_ref[...])
        eig = jnp.concatenate([eig_ref[:, c : c + 2 * side] for c in range(0, side * side, 2 * side)], axis=0)
        eig = eig.T
        eig = jnp.concatenate([eig[:side], eig[side:]], axis=1)
        for j in range(side):
            eig_t_ref[:, j * side : (j + 1) * side] = eig[j : j + 1, :]
        w3_ref[...] = inner_weight(inner_ref[...], side, pack)
        w4_ref[...] = outer_weight(outer_ref[...], side, pack)
        w4t_ref[...] = outer_weight_t(outer_ref[...], side, pack)

    copies[-1].wait()


def prepare(after, tids, qids, eig, inner, outer, x, part, have, devices):
    train, queries, side = tids.shape[1], qids.shape[1], inner.shape[0]
    pack = 256 // side
    wide = side * pack
    return kernel_call(
        functools.partial(prepare_kernel, devices, side, pack, have),
        "prepare",
        (after, tids, qids, eig, inner, outer, x, part),
        [((train, train), BF16), ((queries, queries), BF16), (eig.shape, F32)]
        + [((wide, wide), BF16)] * 3
        + [(x.shape, BF16)],
        [pltpu.SemaphoreType.DMA((1,))],
        [ANYWHERE] + [WHOLE] * 5 + [IN_HBM, WHOLE],
        limit=6 << 20,
        aliases={7: 6},
    )


def query_kernel(side, ahead, after_ref, x_ref, w3_ref, next_any, out_ref, next_ref, last_ref, half_ref, sems):
    rows = next_ref.shape[0]
    copies = fetch((rows_from(next_any, next_ref, 0, rows), (next_any.at[rows : rows + ahead], last_ref.at[:ahead])), sems)
    @beside_fetch
    def _():
        pack = w3_ref.shape[0] // side
        wide = w3_ref.shape[0]
        groups, unit = side // pack, pack * pack
        w3 = w3_ref[...]
        queries = x_ref.shape[0]
        block = min(queries, 256)
        for r in range(0, queries + block, block):
            for g in range(groups):
                if r < queries:
                    part = dot(w3, x_ref[r : r + block, g * wide : (g + 1) * wide], NT).astype(BF16)
                    half_ref[:, g * unit : (g + 1) * unit, r : r + block] = part.reshape(groups, unit, block)
                if r:
                    out_ref[g, r - block : r, :] = half_ref[g, :, r - block : r].T

    for copy in copies:
        copy.wait()


def rotate_query(after, x, w3, upcoming, rows_next, ahead, side):
    rows, feat = x.shape
    wide = w3.shape[0]
    groups = feat // wide
    return kernel_call(
        functools.partial(query_kernel, side, ahead),
        "rotate_query",
        (after, x, w3, upcoming),
        [((groups, rows, wide), BF16), ((rows_next, feat), BF16), ((rows_next, feat), BF16)],
        [pltpu.VMEM((groups, wide, rows), BF16), pltpu.SemaphoreType.DMA((2,))],
        [ANYWHERE, WHOLE, WHOLE, IN_HBM],
        flops=2 * rows * feat * wide,
        limit=12 << 20,
    )


def rotate_rows(side, x_ref, w3_ref, w4_ref, out_ref, half_ref):
    halves(x_ref, w3_ref[...], half_ref, side, w3_ref.shape[0] // side)
    w4 = w4_ref[...]
    for g in range(out_ref.shape[0]):
        out_ref[g] = dot(w4, half_ref[g]).astype(BF16)


def train_kernel(side, after_ref, x_ref, w3_ref, w4_ref, out_ref, half_ref):
    rotate_rows(side, x_ref, w3_ref, w4_ref, out_ref, half_ref)


def train_fetch_kernel(side, have, after_ref, x_ref, w3_ref, w4_ref, next_any, part_ref, out_ref, next_ref, half_ref, sems):
    rows = next_ref.shape[0]
    copies = fetch(((next_any.at[rows + have :], next_ref.at[have:]),), sems)

    @beside_fetch
    def _():
        rotate_rows(side, x_ref, w3_ref, w4_ref, out_ref, half_ref)

    copies[0].wait()


def rotate_train(after, x, w3, w4, side, upcoming=None, part=None, have=0):
    rows, feat = x.shape
    wide = w3.shape[0]
    groups = feat // wide
    body, args, sems, extra = functools.partial(train_kernel, side), (), [], {}
    outs = [((groups, wide, rows), BF16)]
    specs = [ANYWHERE, WHOLE, WHOLE, WHOLE]
    if upcoming is not None:
        body, args = functools.partial(train_fetch_kernel, side, have), (upcoming, part)
        outs.append(((rows, feat), BF16))
        sems = [pltpu.SemaphoreType.DMA((1,))]
        specs += [IN_HBM, WHOLE]
        extra = {"aliases": {5: 1}}
    return kernel_call(
        body,
        "rotate_train",
        (after, x, w3, w4, *args),
        outs,
        [pltpu.VMEM((groups, wide, rows), BF16)] + sems,
        specs,
        flops=4 * rows * feat * wide,
        limit=12 << 20,
        **extra,
    )


def damped_queries(d_ref, hq_ref, w4t_ref, inv, start):
    queries = d_ref.shape[0]
    groups, _, wide = hq_ref.shape
    w4t = w4t_ref[...]
    for g in range(groups):
        d = dot(hq_ref[g, start : start + queries, :], w4t) * inv[:, g * wide : (g + 1) * wide]
        d_ref[:, g * wide : (g + 1) * wide] = d.astype(BF16)


def multiply(p_ref, d_ref, rt_ref, at, inv_cols=()):
    groups, wide, cols = rt_ref.shape
    rt = rt_ref[...].reshape(groups * wide, cols)
    sums = []
    for t in range(0, cols, 256):
        p = dot(d_ref[...], rt[:, t : t + 256])
        if inv_cols:
            sums += self_sums(rt_ref, inv_cols, t, 256)
        hi = p.astype(BF16)
        p_ref[0, :, at + t : at + t + 256] = hi
        p_ref[1, :, at + t : at + t + 256] = (p - hi.astype(F32)).astype(BF16)
    return sums


def select_rows(p_refs, sel_ref, start, out_ref, rows):
    at, got = 0, None
    for p_ref in p_refs:
        cols = p_ref.shape[2]
        pick = sel_ref[start : start + rows, at : at + cols]
        for i in range(2):
            part = dot(pick, p_ref[i], NT)
            got = part if got is None else got + part
        at += cols
    out_ref[:rows, :] = got


def self_sums(rt_ref, inv_cols, at, cols):
    sums = []
    for t in range(at, at + cols, 128):
        acc = jnp.zeros((8, 128), F32)
        for g, col in enumerate(inv_cols):
            r = rt_ref[g, :, t : t + 128].astype(F32)
            acc = acc + (r * r * col[...]).reshape(-1, 8, 128).sum(0)
        sums.append(acc.sum(0, keepdims=True))
    return sums


def on_lines(sums, queries):
    per = queries // 128
    tail = [jnp.concatenate(sums[i : i + per], axis=1) for i in range(0, len(sums), per)]
    tail += [jnp.zeros((1, queries), F32)] * (8 - len(tail))
    return jnp.concatenate(tail, axis=0)


def score_kernel(scale, rta_ref, rtb_ref, hq_ref, eig_ref, sum_ref, w4t_ref, sel_ref, sent_ref, p_ref, tail_ref, d_ref, inv_ref):
    inv = 1.0 / (eig_ref[...] + sum_ref[0:1, 0:1] * scale)
    damped_queries(d_ref, hq_ref, w4t_ref, inv, 0)
    groups, wide, _ = rta_ref.shape
    for g in range(groups):
        inv_ref[g] = jnp.broadcast_to(inv[:, g * wide : (g + 1) * wide], (128, wide)).T
    inv_cols = [inv_ref.at[g] for g in range(groups)]
    sums = multiply(p_ref, d_ref, rta_ref, 0, inv_cols)
    sums += multiply(p_ref, d_ref, rtb_ref, rta_ref.shape[2], inv_cols)
    half = sel_ref.shape[0] // 2
    select_rows((p_ref,), sel_ref, half, sent_ref, half)
    tail = on_lines(sums, sent_ref.shape[1])
    sent_ref[half:, :] = tail
    tail_ref[...] = tail


def partial_scores(rts, hq, eig, eig_sum, w4t, sel, scale, queries):
    train = sel.shape[0]
    feat = eig.shape[1]
    return kernel_call(
        functools.partial(score_kernel, scale),
        "scores_self",
        (*rts, hq, eig, eig_sum, w4t, sel),
        [((train // 2 + 8, queries), F32), ((2, queries, train), BF16), ((8, queries), F32)],
        [pltpu.VMEM((queries, feat), BF16), pltpu.VMEM((*rts[0].shape[:2], 128), F32)],
        limit=16 << 20,
    )


def score_first_kernel(scale, start, after_ref, rt_ref, hq_ref, eig_ref, sum_ref, w4t_ref, d_ref, p_ref):
    inv = 1.0 / (eig_ref[...] + sum_ref[0:1, 0:1] * scale)
    damped_queries(d_ref, hq_ref, w4t_ref, inv, start)
    multiply(p_ref, d_ref, rt_ref, 0)


def score_first(after, rt, hq, eig, eig_sum, w4t, scale, start, queries):
    feat, cols = eig.shape[1], rt.shape[2]
    return kernel_call(
        functools.partial(score_first_kernel, scale, start),
        "scores_first",
        (after, rt, hq, eig, eig_sum, w4t),
        [((queries, feat), BF16), ((2, queries, cols), BF16)],
        (),
        [ANYWHERE] + [WHOLE] * 5,
        limit=8 << 20,
    )


def score_second_kernel(after_ref, rt_ref, d_ref, pa_ref, sel_ref, sent_ref, p_ref):
    multiply(p_ref, d_ref, rt_ref, 0)
    half = sel_ref.shape[0] // 2
    select_rows((pa_ref, p_ref), sel_ref, half, sent_ref, half)


def score_second(after, rt, d, pa, sel):
    queries = d.shape[0]
    train, cols = sel.shape[0], rt.shape[2]
    return kernel_call(
        score_second_kernel,
        "scores_second",
        (after, rt, d, pa, sel),
        [((train // 2, queries), F32), ((2, queries, cols), BF16)],
        (),
        [ANYWHERE] + [WHOLE] * 4,
        limit=8 << 20,
    )


def keep_kernel(start, parts, *refs):
    sel_ref, out_ref = refs[parts + 1], refs[-1]
    rows = sel_ref.shape[0] // 4
    select_rows(refs[1 : parts + 1], sel_ref, start, out_ref, rows)
    if len(refs) > parts + 3:
        out_ref[rows:, :] = refs[parts + 2][...]


def keep_rows(after, ps, sel, later, tail=None):
    queries = ps[0].shape[1]
    rows = sel.shape[0] // 4
    args = (after, *ps, sel) + (() if tail is None else (tail,))
    return kernel_call(
        functools.partial(keep_kernel, 0 if later else rows, len(ps)),
        "keep_later" if later else "keep_first",
        args,
        [((rows + (0 if tail is None else 8), queries), F32)],
        (),
        [ANYWHERE] + [WHOLE] * (len(args) - 1),
        limit=8 << 20,
    )[0]


def pick_queries(scaled, sel):
    hi = scaled.astype(BF16)
    rest = scaled - hi.astype(F32)
    mid = rest.astype(BF16)
    low = (rest - mid.astype(F32)).astype(BF16)
    return dot(hi, sel) + dot(mid, sel) + dot(low, sel)


def finish_first_kernel(mine_ref, got_ref, sel_t_ref, sel_q_ref, out_ref, norm_ref):
    columns = out_ref.shape[0]
    width = mine_ref.shape[1]
    total = mine_ref[...] + got_ref[...]
    train = sel_t_ref.shape[1]
    self_row = jnp.concatenate([total[columns + i : columns + i + 1] for i in range(train // width)], axis=1)
    own = sel_t_ref[: max(columns, 16), :].astype(F32)[:columns]
    norm = lax.rsqrt((own * self_row).sum(1, keepdims=True))
    norm_ref[...] = jnp.broadcast_to(norm, norm_ref.shape)
    out_ref[...] = pick_queries(total[:columns] * norm, sel_q_ref[:width, :])


def finish_second_kernel(mine_ref, got_ref, first_ref, norm_ref, sel_q_ref, out_ref):
    width = mine_ref.shape[1]
    total = (mine_ref[...] + got_ref[...]) * norm_ref[:, 0:1]
    out_ref[...] = first_ref[...] + pick_queries(total, sel_q_ref[sel_q_ref.shape[0] - width :, :])


def finish(first, second, sel_t, sel_q, columns):
    queries = sel_q.shape[0]
    out, norm = kernel_call(
        finish_first_kernel,
        "finish_first",
        (*first, sel_t, sel_q),
        [((columns, queries), F32), ((columns, 128), F32)],
        limit=4 << 20,
    )
    args = [in_vmem(a) for a in (*second, out, norm, sel_q)]
    return pl.pallas_call(
        finish_second_kernel,
        out_shape=jax.ShapeDtypeStruct((columns, queries), F32),
        in_specs=[WHOLE] * len(args),
        out_specs=WHOLE,
        compiler_params=pltpu.CompilerParams(vmem_limit_bytes=4 << 20),
        name="finish_second",
    )(*args)


def sum_kernel(ahead, count, *refs):
    smalls, x_any, out_ref, held, part_ref, sems = refs[:count], refs[count], refs[count + 1], refs[count + 2 : -2], refs[-2], refs[-1]
    copies = fetch((*zip(smalls, held), rows_from(x_any, part_ref, 0, ahead)), sems)
    copies[0].wait()
    x_ref = held[0]
    out_ref[...] = jnp.broadcast_to(jnp.sum(x_ref[...], axis=1, keepdims=True), out_ref.shape)
    for copy in copies[1:]:
        copy.wait()


def next_halves(mine, got, rows):
    total = mine + got
    rows //= 2
    return jnp.concatenate([total[:rows], total[2 * rows :]]), total[rows:]


def halving_step(x, step, devices):
    swap = {1: 2, 2: 1} if devices > 4 else {}
    pairs = [(i, i ^ (1 << (swap.get(step, step) if i % 2 else step))) for i in range(devices)]
    return lax.ppermute(x, "layer", pairs)


def exchange(x, bit, devices):
    return lax.ppermute(x, "layer", [(i, i ^ bit) for i in range(devices)])


def shards(query_pool, train_store, query_ids, train_ids, out_basis, in_basis, eigenvalues):
    devices = lax.axis_size("layer")
    bits = devices.bit_length() - 1
    train = train_store.shape[0]
    queries = query_pool.shape[0]
    side = out_basis.shape[1]
    columns = train // devices
    inner, outer = in_basis[0], out_basis[0]

    scale = 0.1 / (eigenvalues.shape[1] * devices)
    tids, qids = train_ids.reshape(1, train), query_ids.reshape(1, queries)
    xq, xt = query_pool.reshape(queries, -1), train_store.reshape(train, -1)

    half = train // 2
    have_q, have_b = 32, 16
    smalls = (eigenvalues, tids, qids, inner, outer)
    eig_sum, eig_v, tids_v, qids_v, inner_v, outer_v, xq_part = kernel_call(
        functools.partial(sum_kernel, have_q, len(smalls)),
        "eig_sum",
        (*smalls, xq),
        [((1, 128), F32)] + [(a.shape, a.dtype) for a in smalls] + [(xq.shape, BF16)],
        [pltpu.SemaphoreType.DMA((6,))],
        [IN_HBM] * 6,
        limit=1 << 20,
    )
    for b in range(bits):
        got = exchange(eig_sum, 1 << b, devices)
        if b == 0:
            sel_t, sel_q, eig, w3, w4, w4t, xq = prepare(
                eig_sum, tids_v, qids_v, eig_v, inner_v, outer_v, xq, xq_part, have_q, devices
            )
        elif b == 1:
            hq, xa, xb = rotate_query(eig_sum, xq, w3, xt, half, have_b, side)
        elif b == 2:
            rta, xb = rotate_train(eig_sum, xa, w3, w4, side, xt, xb, have_b)
        elif b == 3:
            (rtb,) = rotate_train(eig_sum, xb, w3, w4, side)
        eig_sum = eig_sum + got

    chunk = queries // 2
    sent_a, p_a, tail = partial_scores((rta, rtb), hq, eig, eig_sum, w4t, sel_t, scale, chunk)
    got_a = halving_step(sent_a, 0, devices)
    quarter = half // 2
    first_a = keep_rows(sent_a, [p_a], sel_t, False, tail)
    d, p_b1 = score_first(sent_a, rta, hq, eig, eig_sum, w4t, scale, chunk, chunk)
    sent_a = first_a + got_a[quarter:]
    sent_b, p_b2 = score_second(sent_a, rtb, d, p_b1, sel_t)
    got_b = halving_step(sent_b, 0, devices)
    first_b = keep_rows(sent_b, [p_b1, p_b2], sel_t, False)
    next_a = halving_step(sent_a, 1, devices)
    sent_b = first_b + got_b[quarter:]
    mine_a = keep_rows(sent_b, [p_a], sel_t, True, tail) + jnp.concatenate([got_a[:quarter], got_a[half:]])
    mine_b = keep_rows(sent_b, [p_b1, p_b2], sel_t, True) + got_b[:quarter]
    pairs = [(mine_a, next_a), (mine_b, halving_step(sent_b, 1, devices))]
    for step in range(2, bits):
        for c in range(2):
            mine, sent = next_halves(*pairs[c], half >> (step - 1))
            pairs[c] = (mine, halving_step(sent, step, devices))
    return finish(*pairs, sel_t, sel_q, columns).T


def solution(mesh):
    placed = (
        P("grp", "layer", None),
        P("grp", "layer", None),
        P("grp"),
        P("grp"),
        P("layer", None, None),
        P("layer", None, None),
        P("layer", None),
    )
    return jax.shard_map(
        shards, mesh=mesh, in_specs=placed, out_specs=P("grp", "layer"), check_vma=False
    )
```

```python
import functools

import jax
import jax.numpy as jnp
from jax import lax
from jax.experimental import pallas as pl
from jax.experimental.pallas import tpu as pltpu
from jax.sharding import PartitionSpec as P

BF16 = jnp.bfloat16
F32 = jnp.float32
VMEM_LIMIT = 56 * 1024 * 1024
NN = (((1,), (0,)), ((), ()))
NT = (((1,), (1,)), ((), ()))


def dot(a, b, dims=NN):
    return lax.dot_general(a, b, dims, preferred_element_type=F32)


def iota(shape, dim):
    return lax.broadcasted_iota(jnp.int32, shape, dim)


def onehot(cond):
    return jnp.where(cond, 1.0, 0.0).astype(BF16)


def even_first(place, side):
    return place % (side // 2) * 2 + place // (side // 2)


def inner_weight(basis, side, pack):
    wide = side * pack
    rows = onehot(iota((wide, side), 0) // pack == iota((wide, side), 1))
    cols = onehot(iota((side, wide), 1) % side == iota((side, wide), 0))
    full = dot(dot(rows, basis, NT).astype(BF16), cols)
    keep = iota((wide, wide), 0) % pack == iota((wide, wide), 1) // side
    return jnp.where(keep, full, 0.0).astype(BF16)


def outer_weight(basis, side, pack):
    wide = side * pack
    rows = onehot(even_first(iota((wide, side), 0) % side, side) == iota((wide, side), 1))
    k = iota((side, wide), 1)
    cols = onehot(k // (pack * pack) * pack + k % pack == iota((side, wide), 0))
    full = dot(dot(rows, basis, NT).astype(BF16), cols)
    keep = iota((wide, wide), 0) // side == iota((wide, wide), 1) // pack % pack
    return jnp.where(keep, full, 0.0).astype(BF16)


def outer_weight_t(basis, side, pack):
    wide = side * pack
    k = iota((wide, side), 0)
    rows = onehot(k // (pack * pack) * pack + k % pack == iota((wide, side), 1))
    cols = onehot(even_first(iota((side, wide), 1) % side, side) == iota((side, wide), 0))
    full = dot(dot(rows, basis).astype(BF16), cols)
    keep = iota((wide, wide), 1) // side == iota((wide, wide), 0) // pack % pack
    return jnp.where(keep, full, 0.0).astype(BF16)


def halves(x_ref, weight, half_ref, side, pack):
    wide = side * pack
    groups = side // pack
    unit = pack * pack
    for g in range(groups):
        part = dot(weight, x_ref[:, g * wide : (g + 1) * wide], NT).astype(BF16)
        half_ref[:, g * unit : (g + 1) * unit, :] = part.reshape(groups, unit, part.shape[1])


def in_vmem(x):
    return pltpu.with_memory_space_constraint(x, pltpu.VMEM)


WHOLE = pl.BlockSpec(memory_space=pltpu.VMEM)
IN_HBM = pl.BlockSpec(memory_space=pltpu.HBM)
ANYWHERE = pl.BlockSpec(memory_space=pl.ANY)


def kernel_call(body, name, args, outs, scratch=(), specs=None, flops=0, limit=VMEM_LIMIT, aliases=None):
    specs = specs or [WHOLE] * len(args)
    place = {id(IN_HBM): pltpu.HBM, id(WHOLE): pltpu.VMEM}
    args = [
        pltpu.with_memory_space_constraint(a, place[id(s)]) if id(s) in place and a.size > 2048 or s is IN_HBM else a
        for a, s in zip(args, specs)
    ]
    return pl.pallas_call(
        body,
        out_shape=tuple(pltpu.VMEM(shape, dtype) for shape, dtype in outs),
        in_specs=specs,
        out_specs=tuple([WHOLE] * len(outs)),
        scratch_shapes=list(scratch),
        input_output_aliases=aliases or {},
        compiler_params=pltpu.CompilerParams(vmem_limit_bytes=limit),
        cost_estimate=pl.CostEstimate(flops=flops, bytes_accessed=0, transcendentals=0),
        name=name,
    )(*args)


def fetch(pairs, sems):
    copies = [pltpu.make_async_copy(src, dst, sems.at[i]) for i, (src, dst) in enumerate(pairs)]
    for copy in copies:
        copy.start()
    return copies


def beside_fetch(compute):
    pl.when(lax.axis_index("layer") >= 0)(compute)


def rows_from(x_any, x_ref, start, stop):
    return x_any.at[start:stop], x_ref.at[start:stop]


def swap_bits(ids, low, high, columns, where=True):
    train = ids.shape[1]
    block = iota(ids.shape, 1) // columns
    a, b = (block >> low) & 1, (block >> high) & 1
    shift = ((1 << high) - (1 << low)) * columns
    up, down = pltpu.roll(ids, train - shift, 1), pltpu.roll(ids, shift, 1)
    return jnp.where((a > b) & where, up, jnp.where((a < b) & where, down, ids))


def prepare_kernel(devices, side, pack, have, *refs):
    tids_ref, qids_ref, eig_ref, inner_ref, outer_ref, x_any = refs[1:7]
    sel_t_ref, sel_q_ref, eig_t_ref, w3_ref, w4_ref, w4t_ref, x_ref = refs[8:15]
    copies = fetch((rows_from(x_any, x_ref, have, x_ref.shape[0]),), refs[15])
    @beside_fetch
    def _():
        me = lax.axis_index("layer")
        train, queries = sel_t_ref.shape[0], sel_q_ref.shape[0]
        ids = jnp.broadcast_to(tids_ref[...], (8, train))
        lane = iota((8, train), 1)
        step = train // devices
        core = me % 2
        while step < train:
            bit = (lane // step) % 2
            other = jnp.where(bit == 0, pltpu.roll(ids, train - step, 1), pltpu.roll(ids, step, 1))
            ids = jnp.where(me % 2 == 1, other, ids)
            me = me // 2
            step *= 2
        columns = train // devices
        bits = devices.bit_length() - 1
        if bits > 2:
            ids = swap_bits(ids, 1, 2, columns, (core + lane // columns) % 2 == 1)
        for b in range(bits // 2):
            ids = swap_bits(ids, b, bits - 1 - b, columns)
        for s in range(0, train, 128):
            col = jnp.broadcast_to(ids[0:1, s : s + 128], (128, 128)).T
            for c in range(0, train, 128):
                sel_t_ref[s : s + 128, c : c + 128] = onehot(col == iota((128, 128), 1) + c)
        sel_q_ref[...] = onehot(iota((queries, queries), 0) == qids_ref[...])
        eig = jnp.concatenate([eig_ref[:, c : c + 2 * side] for c in range(0, side * side, 2 * side)], axis=0)
        eig = eig.T
        eig = jnp.concatenate([eig[:side], eig[side:]], axis=1)
        for j in range(side):
            eig_t_ref[:, j * side : (j + 1) * side] = eig[j : j + 1, :]
        w3_ref[...] = inner_weight(inner_ref[...], side, pack)
        w4_ref[...] = outer_weight(outer_ref[...], side, pack)
        w4t_ref[...] = outer_weight_t(outer_ref[...], side, pack)

    copies[-1].wait()


def prepare(after, tids, qids, eig, inner, outer, x, part, have, devices):
    train, queries, side = tids.shape[1], qids.shape[1], inner.shape[0]
    pack = 256 // side
    wide = side * pack
    return kernel_call(
        functools.partial(prepare_kernel, devices, side, pack, have),
        "prepare",
        (after, tids, qids, eig, inner, outer, x, part),
        [((train, train), BF16), ((queries, queries), BF16), (eig.shape, F32)]
        + [((wide, wide), BF16)] * 3
        + [(x.shape, BF16)],
        [pltpu.SemaphoreType.DMA((1,))],
        [ANYWHERE] + [WHOLE] * 5 + [IN_HBM, WHOLE],
        limit=6 << 20,
        aliases={7: 6},
    )


def query_kernel(side, ahead, after_ref, x_ref, w3_ref, w4t_ref, next_any, turned_ref, next_ref, last_ref, half_ref, sems):
    rows = next_ref.shape[0]
    copies = fetch((rows_from(next_any, next_ref, 0, rows), (next_any.at[rows : rows + ahead], last_ref.at[:ahead])), sems)
    @beside_fetch
    def _():
        pack = w3_ref.shape[0] // side
        wide = w3_ref.shape[0]
        groups, unit = side // pack, pack * pack
        w3, w4t = w3_ref[...], w4t_ref[...]
        queries = x_ref.shape[0]
        block = min(queries, 256)
        for r in range(0, queries + block, block):
            for g in range(groups):
                if r < queries:
                    part = dot(w3, x_ref[r : r + block, g * wide : (g + 1) * wide], NT).astype(BF16)
                    half_ref[:, g * unit : (g + 1) * unit, r : r + block] = part.reshape(groups, unit, block)
                if r:
                    turned = half_ref[g, :, r - block : r].T
                    turned_ref[r - block : r, g * wide : (g + 1) * wide] = dot(turned, w4t)

    for copy in copies:
        copy.wait()


def rotate_query(after, x, w3, w4t, upcoming, rows_next, ahead, side):
    rows, feat = x.shape
    wide = w3.shape[0]
    groups = feat // wide
    return kernel_call(
        functools.partial(query_kernel, side, ahead),
        "rotate_query",
        (after, x, w3, w4t, upcoming),
        [((rows, feat), F32), ((rows_next, feat), BF16), ((rows_next, feat), BF16)],
        [pltpu.VMEM((groups, wide, rows), BF16), pltpu.SemaphoreType.DMA((2,))],
        [ANYWHERE, WHOLE, WHOLE, WHOLE, IN_HBM],
        flops=2 * rows * feat * wide,
        limit=12 << 20,
    )


def rotate_rows(side, x_ref, w3_ref, w4_ref, out_ref, half_ref):
    halves(x_ref, w3_ref[...], half_ref, side, w3_ref.shape[0] // side)
    w4 = w4_ref[...]
    for g in range(out_ref.shape[0]):
        out_ref[g] = dot(w4, half_ref[g]).astype(BF16)


def train_kernel(side, after_ref, x_ref, w3_ref, w4_ref, out_ref, half_ref):
    rotate_rows(side, x_ref, w3_ref, w4_ref, out_ref, half_ref)


def train_fetch_kernel(side, have, after_ref, x_ref, w3_ref, w4_ref, next_any, part_ref, out_ref, next_ref, half_ref, sems):
    rows = next_ref.shape[0]
    copies = fetch(((next_any.at[rows + have :], next_ref.at[have:]),), sems)

    @beside_fetch
    def _():
        rotate_rows(side, x_ref, w3_ref, w4_ref, out_ref, half_ref)

    copies[0].wait()


def rotate_train(after, x, w3, w4, side, upcoming=None, part=None, have=0):
    rows, feat = x.shape
    wide = w3.shape[0]
    groups = feat // wide
    body, args, sems, extra = functools.partial(train_kernel, side), (), [], {}
    outs = [((groups, wide, rows), BF16)]
    specs = [ANYWHERE, WHOLE, WHOLE, WHOLE]
    if upcoming is not None:
        body, args = functools.partial(train_fetch_kernel, side, have), (upcoming, part)
        outs.append(((rows, feat), BF16))
        sems = [pltpu.SemaphoreType.DMA((1,))]
        specs += [IN_HBM, WHOLE]
        extra = {"aliases": {5: 1}}
    return kernel_call(
        body,
        "rotate_train",
        (after, x, w3, w4, *args),
        outs,
        [pltpu.VMEM((groups, wide, rows), BF16)] + sems,
        specs,
        flops=4 * rows * feat * wide,
        limit=12 << 20,
        **extra,
    )


def multiply(p_ref, d_ref, rt_ref, at, inv_cols=()):
    groups, wide, cols = rt_ref.shape
    rt = rt_ref[...].reshape(groups * wide, cols)
    sums = []
    for t in range(0, cols, 256):
        p = dot(d_ref[...], rt[:, t : t + 256])
        if inv_cols:
            sums += self_sums(rt_ref, inv_cols, t, 256)
        hi = p.astype(BF16)
        p_ref[0, :, at + t : at + t + 256] = hi
        p_ref[1, :, at + t : at + t + 256] = (p - hi.astype(F32)).astype(BF16)
    return sums


def select_rows(p_refs, sel_ref, start, out_ref, rows):
    at, got = 0, None
    for p_ref in p_refs:
        cols = p_ref.shape[2]
        pick = sel_ref[start : start + rows, at : at + cols]
        for i in range(2):
            part = dot(pick, p_ref[i], NT)
            got = part if got is None else got + part
        at += cols
    out_ref[:rows, :] = got


def self_sums(rt_ref, inv_cols, at, cols):
    sums = []
    for t in range(at, at + cols, 128):
        acc = jnp.zeros((8, 128), F32)
        for g, col in enumerate(inv_cols):
            r = rt_ref[g, :, t : t + 128].astype(F32)
            acc = acc + (r * r * col[...]).reshape(-1, 8, 128).sum(0)
        sums.append(acc.sum(0, keepdims=True))
    return sums


def on_lines(sums, queries):
    per = queries // 128
    tail = [jnp.concatenate(sums[i : i + per], axis=1) for i in range(0, len(sums), per)]
    tail += [jnp.zeros((1, queries), F32)] * (8 - len(tail))
    return jnp.concatenate(tail, axis=0)


def score_kernel(scale, rta_ref, rtb_ref, turned_ref, eig_ref, sum_ref, sel_ref, sent_ref, p_ref, tail_ref, d_ref, inv_ref):
    inv = 1.0 / (eig_ref[...] + sum_ref[0:1, 0:1] * scale)
    d_ref[...] = (turned_ref[: d_ref.shape[0], :] * inv).astype(BF16)
    groups, wide, _ = rta_ref.shape
    for g in range(groups):
        inv_ref[g] = jnp.broadcast_to(inv[:, g * wide : (g + 1) * wide], (128, wide)).T
    inv_cols = [inv_ref.at[g] for g in range(groups)]
    sums = multiply(p_ref, d_ref, rta_ref, 0, inv_cols)
    sums += multiply(p_ref, d_ref, rtb_ref, rta_ref.shape[2], inv_cols)
    half = sel_ref.shape[0] // 2
    select_rows((p_ref,), sel_ref, half, sent_ref, half)
    tail = on_lines(sums, sent_ref.shape[1])
    sent_ref[half:, :] = tail
    tail_ref[...] = tail


def partial_scores(rts, turned, eig, eig_sum, sel, scale, queries):
    train = sel.shape[0]
    feat = turned.shape[1]
    return kernel_call(
        functools.partial(score_kernel, scale),
        "scores_self",
        (*rts, turned, eig, eig_sum, sel),
        [((train // 2 + 8, queries), F32), ((2, queries, train), BF16), ((8, queries), F32)],
        [pltpu.VMEM((queries, feat), BF16), pltpu.VMEM((*rts[0].shape[:2], 128), F32)],
        limit=16 << 20,
    )


def score_first_kernel(scale, start, after_ref, rt_ref, turned_ref, eig_ref, sum_ref, d_ref, p_ref):
    inv = 1.0 / (eig_ref[...] + sum_ref[0:1, 0:1] * scale)
    d_ref[...] = (turned_ref[start : start + d_ref.shape[0], :] * inv).astype(BF16)
    multiply(p_ref, d_ref, rt_ref, 0)


def score_first(after, rt, turned, eig, eig_sum, scale, start, queries):
    feat, cols = eig.shape[1], rt.shape[2]
    return kernel_call(
        functools.partial(score_first_kernel, scale, start),
        "scores_first",
        (after, rt, turned, eig, eig_sum),
        [((queries, feat), BF16), ((2, queries, cols), BF16)],
        (),
        [ANYWHERE] + [WHOLE] * 4,
        limit=8 << 20,
    )


def score_second_kernel(after_ref, rt_ref, d_ref, pa_ref, sel_ref, sent_ref, p_ref):
    multiply(p_ref, d_ref, rt_ref, 0)
    half = sel_ref.shape[0] // 2
    select_rows((pa_ref, p_ref), sel_ref, half, sent_ref, half)


def score_second(after, rt, d, pa, sel):
    queries = d.shape[0]
    train, cols = sel.shape[0], rt.shape[2]
    return kernel_call(
        score_second_kernel,
        "scores_second",
        (after, rt, d, pa, sel),
        [((train // 2, queries), F32), ((2, queries, cols), BF16)],
        (),
        [ANYWHERE] + [WHOLE] * 4,
        limit=8 << 20,
    )


def keep_kernel(start, parts, *refs):
    sel_ref, out_ref = refs[parts + 1], refs[-1]
    rows = sel_ref.shape[0] // 4
    select_rows(refs[1 : parts + 1], sel_ref, start, out_ref, rows)
    if len(refs) > parts + 3:
        out_ref[rows:, :] = refs[parts + 2][...]


def keep_rows(after, ps, sel, later, tail=None):
    queries = ps[0].shape[1]
    rows = sel.shape[0] // 4
    args = (after, *ps, sel) + (() if tail is None else (tail,))
    return kernel_call(
        functools.partial(keep_kernel, 0 if later else rows, len(ps)),
        "keep_later" if later else "keep_first",
        args,
        [((rows + (0 if tail is None else 8), queries), F32)],
        (),
        [ANYWHERE] + [WHOLE] * (len(args) - 1),
        limit=8 << 20,
    )[0]


def pick_queries(scaled, sel):
    hi = scaled.astype(BF16)
    rest = scaled - hi.astype(F32)
    mid = rest.astype(BF16)
    low = (rest - mid.astype(F32)).astype(BF16)
    return dot(hi, sel) + dot(mid, sel) + dot(low, sel)


def finish_first_kernel(mine_ref, got_ref, sel_t_ref, sel_q_ref, out_ref, norm_ref):
    columns = out_ref.shape[0]
    width = mine_ref.shape[1]
    total = mine_ref[...] + got_ref[...]
    train = sel_t_ref.shape[1]
    self_row = jnp.concatenate([total[columns + i : columns + i + 1] for i in range(train // width)], axis=1)
    own = sel_t_ref[: max(columns, 16), :].astype(F32)[:columns]
    norm = lax.rsqrt((own * self_row).sum(1, keepdims=True))
    norm_ref[...] = jnp.broadcast_to(norm, norm_ref.shape)
    out_ref[...] = pick_queries(total[:columns] * norm, sel_q_ref[:width, :])


def finish_second_kernel(mine_ref, got_ref, first_ref, norm_ref, sel_q_ref, out_ref):
    width = mine_ref.shape[1]
    total = (mine_ref[...] + got_ref[...]) * norm_ref[:, 0:1]
    out_ref[...] = first_ref[...] + pick_queries(total, sel_q_ref[sel_q_ref.shape[0] - width :, :])


def finish(first, second, sel_t, sel_q, columns):
    queries = sel_q.shape[0]
    out, norm = kernel_call(
        finish_first_kernel,
        "finish_first",
        (*first, sel_t, sel_q),
        [((columns, queries), F32), ((columns, 128), F32)],
        limit=4 << 20,
    )
    args = [in_vmem(a) for a in (*second, out, norm, sel_q)]
    return pl.pallas_call(
        finish_second_kernel,
        out_shape=jax.ShapeDtypeStruct((columns, queries), F32),
        in_specs=[WHOLE] * len(args),
        out_specs=WHOLE,
        compiler_params=pltpu.CompilerParams(vmem_limit_bytes=4 << 20),
        name="finish_second",
    )(*args)


def sum_kernel(ahead, count, *refs):
    smalls, x_any, out_ref, held, part_ref, sems = refs[:count], refs[count], refs[count + 1], refs[count + 2 : -2], refs[-2], refs[-1]
    copies = fetch((*zip(smalls, held), rows_from(x_any, part_ref, 0, ahead)), sems)
    copies[0].wait()
    x_ref = held[0]
    out_ref[...] = jnp.broadcast_to(jnp.sum(x_ref[...], axis=1, keepdims=True), out_ref.shape)
    for copy in copies[1:]:
        copy.wait()


def next_halves(mine, got, rows):
    total = mine + got
    rows //= 2
    return jnp.concatenate([total[:rows], total[2 * rows :]]), total[rows:]


def halving_step(x, step, devices):
    swap = {1: 2, 2: 1} if devices > 4 else {}
    pairs = [(i, i ^ (1 << (swap.get(step, step) if i % 2 else step))) for i in range(devices)]
    return lax.ppermute(x, "layer", pairs)


def exchange(x, bit, devices):
    return lax.ppermute(x, "layer", [(i, i ^ bit) for i in range(devices)])


def shards(query_pool, train_store, query_ids, train_ids, out_basis, in_basis, eigenvalues):
    devices = lax.axis_size("layer")
    bits = devices.bit_length() - 1
    train = train_store.shape[0]
    queries = query_pool.shape[0]
    side = out_basis.shape[1]
    columns = train // devices
    inner, outer = in_basis[0], out_basis[0]

    scale = 0.1 / (eigenvalues.shape[1] * devices)
    tids, qids = train_ids.reshape(1, train), query_ids.reshape(1, queries)
    xq, xt = query_pool.reshape(queries, -1), train_store.reshape(train, -1)

    half = train // 2
    have_q, have_b = 32, 16
    smalls = (eigenvalues, tids, qids, inner, outer)
    eig_sum, eig_v, tids_v, qids_v, inner_v, outer_v, xq_part = kernel_call(
        functools.partial(sum_kernel, have_q, len(smalls)),
        "eig_sum",
        (*smalls, xq),
        [((1, 128), F32)] + [(a.shape, a.dtype) for a in smalls] + [(xq.shape, BF16)],
        [pltpu.SemaphoreType.DMA((6,))],
        [IN_HBM] * 6,
        limit=1 << 20,
    )
    for b in range(bits):
        got = exchange(eig_sum, 1 << b, devices)
        if b == 0:
            sel_t, sel_q, eig, w3, w4, w4t, xq = prepare(
                eig_sum, tids_v, qids_v, eig_v, inner_v, outer_v, xq, xq_part, have_q, devices
            )
        elif b == 1:
            turned, xa, xb = rotate_query(eig_sum, xq, w3, w4t, xt, half, have_b, side)
        elif b == 2:
            rta, xb = rotate_train(eig_sum, xa, w3, w4, side, xt, xb, have_b)
        elif b == 3:
            (rtb,) = rotate_train(eig_sum, xb, w3, w4, side)
        eig_sum = eig_sum + got

    chunk = queries // 2
    sent_a, p_a, tail = partial_scores((rta, rtb), turned, eig, eig_sum, sel_t, scale, chunk)
    got_a = halving_step(sent_a, 0, devices)
    quarter = half // 2
    first_a = keep_rows(sent_a, [p_a], sel_t, False, tail)
    d, p_b1 = score_first(sent_a, rta, turned, eig, eig_sum, scale, chunk, chunk)
    sent_a = first_a + got_a[quarter:]
    sent_b, p_b2 = score_second(sent_a, rtb, d, p_b1, sel_t)
    got_b = halving_step(sent_b, 0, devices)
    first_b = keep_rows(sent_b, [p_b1, p_b2], sel_t, False)
    next_a = halving_step(sent_a, 1, devices)
    sent_b = first_b + got_b[quarter:]
    mine_a = keep_rows(sent_b, [p_a], sel_t, True, tail) + jnp.concatenate([got_a[:quarter], got_a[half:]])
    mine_b = keep_rows(sent_b, [p_b1, p_b2], sel_t, True) + got_b[:quarter]
    pairs = [(mine_a, next_a), (mine_b, halving_step(sent_b, 1, devices))]
    for step in range(2, bits):
        for c in range(2):
            mine, sent = next_halves(*pairs[c], half >> (step - 1))
            pairs[c] = (mine, halving_step(sent, step, devices))
    return finish(*pairs, sel_t, sel_q, columns).T


def solution(mesh):
    placed = (
        P("grp", "layer", None),
        P("grp", "layer", None),
        P("grp"),
        P("grp"),
        P("layer", None, None),
        P("layer", None, None),
        P("layer", None),
    )
    return jax.shard_map(
        shards, mesh=mesh, in_specs=placed, out_specs=P("grp", "layer"), check_vma=False
    )
```

```python
import functools

import jax
import jax.numpy as jnp
from jax import lax
from jax.experimental import pallas as pl
from jax.experimental.pallas import tpu as pltpu
from jax.sharding import PartitionSpec as P

BF16 = jnp.bfloat16
F32 = jnp.float32
VMEM_LIMIT = 56 * 1024 * 1024
NN = (((1,), (0,)), ((), ()))
NT = (((1,), (1,)), ((), ()))


def dot(a, b, dims=NN):
    return lax.dot_general(a, b, dims, preferred_element_type=F32)


def iota(shape, dim):
    return lax.broadcasted_iota(jnp.int32, shape, dim)


def onehot(cond):
    return jnp.where(cond, 1.0, 0.0).astype(BF16)


def even_first(place, side):
    return place % (side // 2) * 2 + place // (side // 2)


def inner_weight(basis, side, pack):
    wide = side * pack
    rows = onehot(iota((wide, side), 0) // pack == iota((wide, side), 1))
    cols = onehot(iota((side, wide), 1) % side == iota((side, wide), 0))
    full = dot(dot(rows, basis, NT).astype(BF16), cols)
    keep = iota((wide, wide), 0) % pack == iota((wide, wide), 1) // side
    return jnp.where(keep, full, 0.0).astype(BF16)


def outer_weight(basis, side, pack):
    wide = side * pack
    rows = onehot(even_first(iota((wide, side), 0) % side, side) == iota((wide, side), 1))
    k = iota((side, wide), 1)
    cols = onehot(k // (pack * pack) * pack + k % pack == iota((side, wide), 0))
    full = dot(dot(rows, basis, NT).astype(BF16), cols)
    keep = iota((wide, wide), 0) // side == iota((wide, wide), 1) // pack % pack
    return jnp.where(keep, full, 0.0).astype(BF16)


def outer_weight_t(basis, side, pack):
    wide = side * pack
    k = iota((wide, side), 0)
    rows = onehot(k // (pack * pack) * pack + k % pack == iota((wide, side), 1))
    cols = onehot(even_first(iota((side, wide), 1) % side, side) == iota((side, wide), 0))
    full = dot(dot(rows, basis).astype(BF16), cols)
    keep = iota((wide, wide), 1) // side == iota((wide, wide), 0) // pack % pack
    return jnp.where(keep, full, 0.0).astype(BF16)


def halves(x_ref, weight, half_ref, side, pack):
    wide = side * pack
    groups = side // pack
    unit = pack * pack
    for g in range(groups):
        part = dot(weight, x_ref[:, g * wide : (g + 1) * wide], NT).astype(BF16)
        half_ref[:, g * unit : (g + 1) * unit, :] = part.reshape(groups, unit, part.shape[1])


def in_vmem(x):
    return pltpu.with_memory_space_constraint(x, pltpu.VMEM)


WHOLE = pl.BlockSpec(memory_space=pltpu.VMEM)
IN_HBM = pl.BlockSpec(memory_space=pltpu.HBM)
ANYWHERE = pl.BlockSpec(memory_space=pl.ANY)


def kernel_call(body, name, args, outs, scratch=(), specs=None, flops=0, limit=VMEM_LIMIT, aliases=None):
    specs = specs or [WHOLE] * len(args)
    place = {id(IN_HBM): pltpu.HBM, id(WHOLE): pltpu.VMEM}
    args = [
        pltpu.with_memory_space_constraint(a, place[id(s)]) if id(s) in place and a.size > 2048 or s is IN_HBM else a
        for a, s in zip(args, specs)
    ]
    return pl.pallas_call(
        body,
        out_shape=tuple(pltpu.VMEM(shape, dtype) for shape, dtype in outs),
        in_specs=specs,
        out_specs=tuple([WHOLE] * len(outs)),
        scratch_shapes=list(scratch),
        input_output_aliases=aliases or {},
        compiler_params=pltpu.CompilerParams(vmem_limit_bytes=limit),
        cost_estimate=pl.CostEstimate(flops=flops, bytes_accessed=0, transcendentals=0),
        name=name,
    )(*args)


def fetch(pairs, sems):
    copies = [pltpu.make_async_copy(src, dst, sems.at[i]) for i, (src, dst) in enumerate(pairs)]
    for copy in copies:
        copy.start()
    return copies


def beside_fetch(compute):
    pl.when(lax.axis_index("layer") >= 0)(compute)


def rows_from(x_any, x_ref, start, stop):
    return x_any.at[start:stop], x_ref.at[start:stop]


def swap_bits(ids, low, high, columns, where=True):
    train = ids.shape[1]
    block = iota(ids.shape, 1) // columns
    a, b = (block >> low) & 1, (block >> high) & 1
    shift = ((1 << high) - (1 << low)) * columns
    up, down = pltpu.roll(ids, train - shift, 1), pltpu.roll(ids, shift, 1)
    return jnp.where((a > b) & where, up, jnp.where((a < b) & where, down, ids))


def prepare_kernel(devices, side, pack, have, *refs):
    tids_ref, qids_ref, eig_ref, inner_ref, outer_ref, x_any = refs[1:7]
    sel_t_ref, sel_q_ref, eig_t_ref, w3_ref, w4_ref, w4t_ref, x_ref = refs[8:15]
    copies = fetch((rows_from(x_any, x_ref, have, x_ref.shape[0]),), refs[15])
    @beside_fetch
    def _():
        me = lax.axis_index("layer")
        train, queries = sel_t_ref.shape[0], sel_q_ref.shape[0]
        ids = jnp.broadcast_to(tids_ref[...], (8, train))
        lane = iota((8, train), 1)
        step = train // devices
        core = me % 2
        while step < train:
            bit = (lane // step) % 2
            other = jnp.where(bit == 0, pltpu.roll(ids, train - step, 1), pltpu.roll(ids, step, 1))
            ids = jnp.where(me % 2 == 1, other, ids)
            me = me // 2
            step *= 2
        columns = train // devices
        bits = devices.bit_length() - 1
        if bits > 2:
            ids = swap_bits(ids, 1, 2, columns, (core + lane // columns) % 2 == 1)
        for b in range(bits // 2):
            ids = swap_bits(ids, b, bits - 1 - b, columns)
        for s in range(0, train, 128):
            col = jnp.broadcast_to(ids[0:1, s : s + 128], (128, 128)).T
            for c in range(0, train, 128):
                sel_t_ref[s : s + 128, c : c + 128] = onehot(col == iota((128, 128), 1) + c)
        sel_q_ref[...] = onehot(iota((queries, queries), 0) == qids_ref[...])
        eig = jnp.concatenate([eig_ref[:, c : c + 2 * side] for c in range(0, side * side, 2 * side)], axis=0)
        eig = eig.T
        eig = jnp.concatenate([eig[:side], eig[side:]], axis=1)
        for j in range(side):
            eig_t_ref[:, j * side : (j + 1) * side] = eig[j : j + 1, :]
        w3_ref[...] = inner_weight(inner_ref[...], side, pack)
        w4_ref[...] = outer_weight(outer_ref[...], side, pack)
        w4t_ref[...] = outer_weight_t(outer_ref[...], side, pack)

    copies[-1].wait()


def prepare(after, tids, qids, eig, inner, outer, x, part, have, devices):
    train, queries, side = tids.shape[1], qids.shape[1], inner.shape[0]
    pack = 256 // side
    wide = side * pack
    return kernel_call(
        functools.partial(prepare_kernel, devices, side, pack, have),
        "prepare",
        (after, tids, qids, eig, inner, outer, x, part),
        [((train, train), BF16), ((queries, queries), BF16), (eig.shape, F32)]
        + [((wide, wide), BF16)] * 3
        + [(x.shape, BF16)],
        [pltpu.SemaphoreType.DMA((1,))],
        [ANYWHERE] + [WHOLE] * 5 + [IN_HBM, WHOLE],
        limit=6 << 20,
        aliases={7: 6},
    )


def query_kernel(side, ahead, after_ref, x_ref, w3_ref, w4t_ref, next_any, turned_ref, next_ref, last_ref, half_ref, sems):
    rows = next_ref.shape[0]
    copies = fetch((rows_from(next_any, next_ref, 0, rows), (next_any.at[rows : rows + ahead], last_ref.at[:ahead])), sems)
    @beside_fetch
    def _():
        pack = w3_ref.shape[0] // side
        wide = w3_ref.shape[0]
        groups, unit = side // pack, pack * pack
        w3, w4t = w3_ref[...], w4t_ref[...]
        queries = x_ref.shape[0]
        block = min(queries, 256)
        for r in range(0, queries + block, block):
            for g in range(groups):
                if r < queries:
                    part = dot(w3, x_ref[r : r + block, g * wide : (g + 1) * wide], NT).astype(BF16)
                    half_ref[:, g * unit : (g + 1) * unit, r : r + block] = part.reshape(groups, unit, block)
                if r:
                    turned = half_ref[g, :, r - block : r].T
                    turned_ref[r - block : r, g * wide : (g + 1) * wide] = dot(turned, w4t)

    for copy in copies:
        copy.wait()


def rotate_query(after, x, w3, w4t, upcoming, rows_next, ahead, side):
    rows, feat = x.shape
    wide = w3.shape[0]
    groups = feat // wide
    return kernel_call(
        functools.partial(query_kernel, side, ahead),
        "rotate_query",
        (after, x, w3, w4t, upcoming),
        [((rows, feat), F32), ((rows_next, feat), BF16), ((rows_next, feat), BF16)],
        [pltpu.VMEM((groups, wide, rows), BF16), pltpu.SemaphoreType.DMA((2,))],
        [ANYWHERE, WHOLE, WHOLE, WHOLE, IN_HBM],
        flops=2 * rows * feat * wide,
        limit=12 << 20,
    )


def rotate_rows(side, x_ref, w3_ref, w4_ref, out_ref, half_ref):
    halves(x_ref, w3_ref[...], half_ref, side, w3_ref.shape[0] // side)
    w4 = w4_ref[...]
    for g in range(out_ref.shape[0]):
        out_ref[g] = dot(w4, half_ref[g]).astype(BF16)


def train_kernel(side, after_ref, x_ref, w3_ref, w4_ref, out_ref, half_ref):
    rotate_rows(side, x_ref, w3_ref, w4_ref, out_ref, half_ref)


def train_fetch_kernel(side, have, after_ref, x_ref, w3_ref, w4_ref, next_any, part_ref, out_ref, next_ref, half_ref, sems):
    rows = next_ref.shape[0]
    copies = fetch(((next_any.at[rows + have :], next_ref.at[have:]),), sems)

    @beside_fetch
    def _():
        rotate_rows(side, x_ref, w3_ref, w4_ref, out_ref, half_ref)

    copies[0].wait()


def rotate_train(after, x, w3, w4, side, upcoming=None, part=None, have=0):
    rows, feat = x.shape
    wide = w3.shape[0]
    groups = feat // wide
    body, args, sems, extra = functools.partial(train_kernel, side), (), [], {}
    outs = [((groups, wide, rows), BF16)]
    specs = [ANYWHERE, WHOLE, WHOLE, WHOLE]
    if upcoming is not None:
        body, args = functools.partial(train_fetch_kernel, side, have), (upcoming, part)
        outs.append(((rows, feat), BF16))
        sems = [pltpu.SemaphoreType.DMA((1,))]
        specs += [IN_HBM, WHOLE]
        extra = {"aliases": {5: 1}}
    return kernel_call(
        body,
        "rotate_train",
        (after, x, w3, w4, *args),
        outs,
        [pltpu.VMEM((groups, wide, rows), BF16)] + sems,
        specs,
        flops=4 * rows * feat * wide,
        limit=12 << 20,
        **extra,
    )


def multiply(p_ref, d_ref, rt_ref, at, inv_cols=()):
    groups, wide, cols = rt_ref.shape
    rt = rt_ref[...].reshape(groups * wide, cols)
    sums = []
    for t in range(0, cols, 256):
        p = dot(d_ref[...], rt[:, t : t + 256])
        if inv_cols:
            sums += self_sums(rt_ref, inv_cols, t, 256)
        hi = p.astype(BF16)
        p_ref[0, :, at + t : at + t + 256] = hi
        p_ref[1, :, at + t : at + t + 256] = (p - hi.astype(F32)).astype(BF16)
    return sums


def select_rows(p_refs, sel_ref, start, out_ref, rows):
    at, got = 0, None
    for p_ref in p_refs:
        cols = p_ref.shape[2]
        pick = sel_ref[start : start + rows, at : at + cols]
        for i in range(2):
            part = dot(pick, p_ref[i], NT)
            got = part if got is None else got + part
        at += cols
    out_ref[:rows, :] = got


def self_sums(rt_ref, inv_cols, at, cols):
    sums = []
    for t in range(at, at + cols, 128):
        acc = jnp.zeros((8, 128), F32)
        for g, col in enumerate(inv_cols):
            r = rt_ref[g, :, t : t + 128].astype(F32)
            acc = acc + (r * r * col[...]).reshape(-1, 8, 128).sum(0)
        sums.append(acc.sum(0, keepdims=True))
    return sums


def on_lines(sums, queries):
    per = queries // 128
    tail = [jnp.concatenate(sums[i : i + per], axis=1) for i in range(0, len(sums), per)]
    tail += [jnp.zeros((1, queries), F32)] * (8 - len(tail))
    return jnp.concatenate(tail, axis=0)


def score_kernel(scale, rta_ref, rtb_ref, turned_ref, eig_ref, sum_ref, sel_ref, sent_ref, p_ref, tail_ref, d_ref, inv_ref):
    inv = 1.0 / (eig_ref[...] + sum_ref[0:1, 0:1] * scale)
    d_ref[...] = (turned_ref[: d_ref.shape[0], :] * inv).astype(BF16)
    groups, wide, _ = rta_ref.shape
    for g in range(groups):
        inv_ref[g] = jnp.broadcast_to(inv[:, g * wide : (g + 1) * wide], (128, wide)).T
    inv_cols = [inv_ref.at[g] for g in range(groups)]
    sums = multiply(p_ref, d_ref, rta_ref, 0, inv_cols)
    sums += multiply(p_ref, d_ref, rtb_ref, rta_ref.shape[2], inv_cols)
    half = sel_ref.shape[0] // 2
    select_rows((p_ref,), sel_ref, half, sent_ref, half)
    tail = on_lines(sums, sent_ref.shape[1])
    sent_ref[half:, :] = tail
    tail_ref[...] = tail


def partial_scores(rts, turned, eig, eig_sum, sel, scale, queries):
    train = sel.shape[0]
    feat = turned.shape[1]
    return kernel_call(
        functools.partial(score_kernel, scale),
        "scores_self",
        (*rts, turned, eig, eig_sum, sel),
        [((train // 2 + 8, queries), F32), ((2, queries, train), BF16), ((8, queries), F32)],
        [pltpu.VMEM((queries, feat), BF16), pltpu.VMEM((*rts[0].shape[:2], 128), F32)],
        limit=16 << 20,
    )


def score_first_kernel(scale, start, after_ref, rt_ref, turned_ref, eig_ref, sum_ref, d_ref, p_ref):
    inv = 1.0 / (eig_ref[...] + sum_ref[0:1, 0:1] * scale)
    d_ref[...] = (turned_ref[start : start + d_ref.shape[0], :] * inv).astype(BF16)
    multiply(p_ref, d_ref, rt_ref, 0)


def score_first(after, rt, turned, eig, eig_sum, scale, start, queries):
    feat, cols = eig.shape[1], rt.shape[2]
    return kernel_call(
        functools.partial(score_first_kernel, scale, start),
        "scores_first",
        (after, rt, turned, eig, eig_sum),
        [((queries, feat), BF16), ((2, queries, cols), BF16)],
        (),
        [ANYWHERE] + [WHOLE] * 4,
        limit=8 << 20,
    )


def score_second_kernel(after_ref, rt_ref, d_ref, pa_ref, sel_ref, sent_ref, p_ref):
    multiply(p_ref, d_ref, rt_ref, 0)
    half = sel_ref.shape[0] // 2
    select_rows((pa_ref, p_ref), sel_ref, half, sent_ref, half)


def score_second(after, rt, d, pa, sel):
    queries = d.shape[0]
    train, cols = sel.shape[0], rt.shape[2]
    return kernel_call(
        score_second_kernel,
        "scores_second",
        (after, rt, d, pa, sel),
        [((train // 2, queries), F32), ((2, queries, cols), BF16)],
        (),
        [ANYWHERE] + [WHOLE] * 4,
        limit=8 << 20,
    )


def keep_kernel(start, parts, *refs):
    sel_ref, out_ref = refs[parts + 1], refs[-1]
    rows = sel_ref.shape[0] // 4
    select_rows(refs[1 : parts + 1], sel_ref, start, out_ref, rows)
    if len(refs) > parts + 3:
        out_ref[rows:, :] = refs[parts + 2][...]


def keep_rows(after, ps, sel, later, tail=None):
    queries = ps[0].shape[1]
    rows = sel.shape[0] // 4
    args = (after, *ps, sel) + (() if tail is None else (tail,))
    return kernel_call(
        functools.partial(keep_kernel, 0 if later else rows, len(ps)),
        "keep_later" if later else "keep_first",
        args,
        [((rows + (0 if tail is None else 8), queries), F32)],
        (),
        [ANYWHERE] + [WHOLE] * (len(args) - 1),
        limit=8 << 20,
    )[0]


def pick_queries(scaled, sel):
    hi = scaled.astype(BF16)
    low = (scaled - hi.astype(F32)).astype(BF16)
    return dot(hi, sel) + dot(low, sel)


def finish_first_kernel(mine_ref, got_ref, sel_t_ref, sel_q_ref, out_ref, norm_ref):
    columns = out_ref.shape[0]
    width = mine_ref.shape[1]
    total = mine_ref[...] + got_ref[...]
    train = sel_t_ref.shape[1]
    self_row = jnp.concatenate([total[columns + i : columns + i + 1] for i in range(train // width)], axis=1)
    own = sel_t_ref[: max(columns, 16), :].astype(F32)[:columns]
    norm = lax.rsqrt((own * self_row).sum(1, keepdims=True))
    norm_ref[...] = jnp.broadcast_to(norm, norm_ref.shape)
    out_ref[...] = pick_queries(total[:columns] * norm, sel_q_ref[:width, :])


def finish_second_kernel(mine_ref, got_ref, first_ref, norm_ref, sel_q_ref, out_ref):
    width = mine_ref.shape[1]
    total = (mine_ref[...] + got_ref[...]) * norm_ref[:, 0:1]
    out_ref[...] = first_ref[...] + pick_queries(total, sel_q_ref[sel_q_ref.shape[0] - width :, :])


def finish(first, second, sel_t, sel_q, columns):
    queries = sel_q.shape[0]
    out, norm = kernel_call(
        finish_first_kernel,
        "finish_first",
        (*first, sel_t, sel_q),
        [((columns, queries), F32), ((columns, 128), F32)],
        limit=4 << 20,
    )
    args = [in_vmem(a) for a in (*second, out, norm, sel_q)]
    return pl.pallas_call(
        finish_second_kernel,
        out_shape=jax.ShapeDtypeStruct((columns, queries), F32),
        in_specs=[WHOLE] * len(args),
        out_specs=WHOLE,
        compiler_params=pltpu.CompilerParams(vmem_limit_bytes=4 << 20),
        name="finish_second",
    )(*args)


def sum_kernel(ahead, count, *refs):
    smalls, x_any, out_ref, held, part_ref, sems = refs[:count], refs[count], refs[count + 1], refs[count + 2 : -2], refs[-2], refs[-1]
    copies = fetch((*zip(smalls, held), rows_from(x_any, part_ref, 0, ahead)), sems)
    copies[0].wait()
    x_ref = held[0]
    out_ref[...] = jnp.broadcast_to(jnp.sum(x_ref[...], axis=1, keepdims=True), out_ref.shape)
    for copy in copies[1:]:
        copy.wait()


def next_halves(mine, got, rows):
    total = mine + got
    rows //= 2
    return jnp.concatenate([total[:rows], total[2 * rows :]]), total[rows:]


def halving_step(x, step, devices):
    swap = {1: 2, 2: 1} if devices > 4 else {}
    pairs = [(i, i ^ (1 << (swap.get(step, step) if i % 2 else step))) for i in range(devices)]
    return lax.ppermute(x, "layer", pairs)


def exchange(x, bit, devices):
    return lax.ppermute(x, "layer", [(i, i ^ bit) for i in range(devices)])


def shards(query_pool, train_store, query_ids, train_ids, out_basis, in_basis, eigenvalues):
    devices = lax.axis_size("layer")
    bits = devices.bit_length() - 1
    train = train_store.shape[0]
    queries = query_pool.shape[0]
    side = out_basis.shape[1]
    columns = train // devices
    inner, outer = in_basis[0], out_basis[0]

    scale = 0.1 / (eigenvalues.shape[1] * devices)
    tids, qids = train_ids.reshape(1, train), query_ids.reshape(1, queries)
    xq, xt = query_pool.reshape(queries, -1), train_store.reshape(train, -1)

    half = train // 2
    have_q, have_b = 32, 112
    smalls = (eigenvalues, tids, qids, inner, outer)
    eig_sum, eig_v, tids_v, qids_v, inner_v, outer_v, xq_part = kernel_call(
        functools.partial(sum_kernel, have_q, len(smalls)),
        "eig_sum",
        (*smalls, xq),
        [((1, 128), F32)] + [(a.shape, a.dtype) for a in smalls] + [(xq.shape, BF16)],
        [pltpu.SemaphoreType.DMA((6,))],
        [IN_HBM] * 6,
        limit=1 << 20,
    )
    for b in range(bits):
        got = exchange(eig_sum, 1 << b, devices)
        if b == 0:
            sel_t, sel_q, eig, w3, w4, w4t, xq = prepare(
                eig_sum, tids_v, qids_v, eig_v, inner_v, outer_v, xq, xq_part, have_q, devices
            )
        elif b == 1:
            turned, xa, xb = rotate_query(eig_sum, xq, w3, w4t, xt, half, have_b, side)
        elif b == 2:
            rta, xb = rotate_train(eig_sum, xa, w3, w4, side, xt, xb, have_b)
        elif b == 3:
            (rtb,) = rotate_train(eig_sum, xb, w3, w4, side)
        eig_sum = eig_sum + got

    chunk = queries // 2
    sent_a, p_a, tail = partial_scores((rta, rtb), turned, eig, eig_sum, sel_t, scale, chunk)
    got_a = halving_step(sent_a, 0, devices)
    quarter = half // 2
    first_a = keep_rows(sent_a, [p_a], sel_t, False, tail)
    d, p_b1 = score_first(sent_a, rta, turned, eig, eig_sum, scale, chunk, chunk)
    sent_a = first_a + got_a[quarter:]
    sent_b, p_b2 = score_second(sent_a, rtb, d, p_b1, sel_t)
    got_b = halving_step(sent_b, 0, devices)
    first_b = keep_rows(sent_b, [p_b1, p_b2], sel_t, False)
    next_a = halving_step(sent_a, 1, devices)
    sent_b = first_b + got_b[quarter:]
    mine_a = keep_rows(sent_b, [p_a], sel_t, True, tail) + jnp.concatenate([got_a[:quarter], got_a[half:]])
    mine_b = keep_rows(sent_b, [p_b1, p_b2], sel_t, True) + got_b[:quarter]
    pairs = [(mine_a, next_a), (mine_b, halving_step(sent_b, 1, devices))]
    for step in range(2, bits):
        for c in range(2):
            mine, sent = next_halves(*pairs[c], half >> (step - 1))
            pairs[c] = (mine, halving_step(sent, step, devices))
    return finish(*pairs, sel_t, sel_q, columns).T


def solution(mesh):
    placed = (
        P("grp", "layer", None),
        P("grp", "layer", None),
        P("grp"),
        P("grp"),
        P("layer", None, None),
        P("layer", None, None),
        P("layer", None),
    )
    return jax.shard_map(
        shards, mesh=mesh, in_specs=placed, out_specs=P("grp", "layer"), check_vma=False
    )
```
